128 devices in a mesh: gx: 8 (over z_lo, y), gy: 8 (over x, core), gz: 2 (over z_hi).
Axes of the slice: x: 4, y: 4, z: 4 (z_hi: 2, z_lo: 2; z = z_hi * 2 + z_lo), core: 2. Of those that a mesh axis runs over, the one named last changes fastest.
Arguments:
- pressure: float32 [256, 256, 256], P('gx', 'gy', 'gz'), may hold values from -2.5 to 2.5
- source: float32 [256, 256, 256], P('gx', 'gy', 'gz'), may hold values from -40 to 40
- saturation: float32 [256, 256, 256], P('gx', 'gy', 'gz'), may hold values from 0.1 to 0.9
- permeability: float32 [256, 256, 256], P('gx', 'gy', 'gz'), may hold values from 0.1 to 10
- compress: float32 [256, 256, 256], P('gx', 'gy', 'gz'), may hold values from 0.1 to 1
- porosity: float32 [256, 256, 256], P('gx', 'gy', 'gz'), may hold values from 0.1 to 0.3
- rock_type: int32 [256, 256, 256], P('gx', 'gy', 'gz'), may hold values from 0 to 7
- well_mask: int32 [256, 256, 256], P('gx', 'gy', 'gz'), may hold values 0 or 1
- oil_factor: float32 [8], replicated, may hold values from 0.3 to 3
Outputs:
- pressure_new: float32 [256, 256, 256], P('gx', 'gy', 'gz')
- residual_new: float32 [256, 256, 256], P('gx', 'gy', 'gz')
- saturation_new: float32 [256, 256, 256], P('gx', 'gy', 'gz')
The draws below stay inside these ranges and needn't reach their ends.
All inputs are finite; a program needn't handle non-finite values. No bound on the sum of `well_mask` on one device may be relied on, other than what follows from the above.
Results may differ from the reference program's by a relative error of at most 0.0003.
Values sent between devices are 32-bit elements; how exact they have to be, the bound alone decides.
A program may use at most 64 MiB of HBM per device.

```python
import math
import jax
import jax.numpy as jnp
from jax import lax

CX = 32
CY = 32
CZ = 128
INTERSECTION = 8
NEWTON = 3
ROCKS = 8
NX = 256
NY = 256
NZ = 256
N_GX = 8
N_GY = 8
N_GZ = 2


def draw_source(key, part):
    key_base, key_x, key_y = jax.random.split(jax.random.fold_in(key, 11), 3)
    scale_x = 0.1 * jnp.exp(jax.random.uniform(key_x, (NX,), jnp.float32, 0.0, math.log(10.0)))
    scale_y = 0.1 * jnp.exp(jax.random.uniform(key_y, (NY,), jnp.float32, 0.0, math.log(10.0)))
    base_vals = jnp.clip(jax.random.normal(key_base, (NX, NY, NZ), jnp.float32), -4.0, 4.0)
    return base_vals * (scale_x[:, None, None] * 10.0) * scale_y[None, :, None]


def touch_ends(values, stream_key, low, top_value):
    shape = values.shape
    place = [jax.random.randint(jax.random.fold_in(stream_key, axis), (), 0, shape[axis]) for axis in range(len(shape))]
    values = values.at[tuple(place)].set(low)
    longest = shape.index(max(shape))
    place[longest] = (place[longest] + 1) % shape[longest]
    return values.at[tuple(place)].set(top_value)


def steps_of(rng, dims, cuts, low, high):
    gain = 1.0
    for axis_at, blocks in cuts:
        steps = jax.random.uniform(jax.random.fold_in(jax.random.fold_in(rng, 6), axis_at), (blocks,), jnp.float32, low / len(cuts), high / len(cuts))
        gain = gain * jnp.repeat(jnp.exp(steps), dims[axis_at] // blocks).reshape((-1,) + (1,) * (len(dims) - 1 - axis_at))
    return gain


def normal_values(rng, extent, deviation, limit, shards=(), kind=jnp.bfloat16):
    values = jax.random.normal(rng, extent, jnp.float32) * deviation
    if len(shards) > 0:
        values = steps_of(rng, extent, shards, -0.22, 0.18) * values
    return jnp.clip(values, min=-limit, max=limit).astype(kind)


def setup_inputs(seed: int = 0) -> dict:
    keys = jax.random.split(jax.random.key(seed), 10)
    pressure = normal_values(keys[0], (NX, NY, NZ), 0.3, 2.5, ((0, 8), (1, 8), (2, 2)), jnp.float32)
    source = draw_source(jax.random.fold_in(keys[9], 71), 0)
    saturation = jnp.clip(0.1 + 0.79999997 * jax.random.uniform(keys[2], (NX, NY, NZ), jnp.float32) ** steps_of(keys[2], (NX, NY, NZ), ((0, 8), (1, 8), (2, 2)), -0.2, 0.2), 0.1, 0.9)
    permeability = jnp.clip(jnp.exp(math.log(10.0) - 4.6051702 * jax.random.uniform(keys[3], (NX, NY, NZ), jnp.float32) ** steps_of(keys[3], (NX, NY, NZ), ((0, 8), (1, 8), (2, 2)), -0.2, 0.2)), 0.1, 10.0)
    compress = jnp.clip(jnp.exp(math.log(1.0) - 2.3025851 * jax.random.uniform(keys[4], (NX, NY, NZ), jnp.float32) ** steps_of(keys[4], (NX, NY, NZ), ((0, 8), (1, 8), (2, 2)), -0.2, 0.2)), 0.1, 1.0)
    porosity = jnp.clip(0.1 + 0.20000001043081284 * jax.random.uniform(keys[5], (NX, NY, NZ), jnp.float32) ** steps_of(keys[5], (NX, NY, NZ), ((0, 8), (1, 8), (2, 2)), -0.2, 0.2), 0.1, 0.3)
    rock_type = touch_ends(jax.random.randint(keys[6], (NX, NY, NZ), 0, ROCKS), jax.random.fold_in(keys[6], 1), 0, ROCKS - 1).astype(jnp.int32)
    well_mask = touch_ends((jax.random.randint(keys[7], (NX, NY, NZ), 0, 32) < 1).astype(jnp.int32), jax.random.fold_in(keys[7], 1), 0, 1)
    oil_factor = jnp.clip(jnp.exp(jax.random.uniform(keys[8], (ROCKS,), jnp.float32, math.log(0.3), math.log(3.0))), 0.3, 3.0)
    return dict(pressure=pressure, source=source, saturation=saturation, permeability=permeability, compress=compress, porosity=porosity, rock_type=rock_type, well_mask=well_mask, oil_factor=oil_factor)


WELL_INDEX = 4.0
INJECT_RATE = 2.0
TIME_STEP = 0.05

def sine_basis(length):
    points = jnp.arange(length, dtype=jnp.int32) + 1
    product = points[:, None] * points[None, :] % (2 * (length + 1))
    angles = product.astype(jnp.float32) * (math.pi / (length + 1))
    sine_table = math.sqrt(2.0 / (length + 1)) * jnp.sin(angles)
    eigen_vals = 2.0 - 2.0 * jnp.cos(points.astype(jnp.float32) * (math.pi / (length + 1)))
    return (sine_table, eigen_vals)

def solve_box(box_field):
    basis_x, eigen_x = sine_basis(box_field.shape[0])
    basis_y, eigen_y = sine_basis(box_field.shape[1])
    basis_z, eigen_z = sine_basis(box_field.shape[2])
    precise = lax.Precision.HIGHEST
    spectral = jnp.einsum('ai,ijk->ajk', basis_x, box_field, precision=precise)
    spectral = jnp.einsum('bj,ajk->abk', basis_y, spectral, precision=precise)
    spectral = jnp.einsum('ck,abk->abc', basis_z, spectral, precision=precise)
    spectral = spectral / (eigen_x[:, None, None] + eigen_y[None, :, None] + eigen_z[None, None, :])
    spectral = jnp.einsum('ai,ijk->ajk', basis_x, spectral, precision=precise)
    spectral = jnp.einsum('bj,ajk->abk', basis_y, spectral, precision=precise)
    spectral = jnp.einsum('ck,abk->abc', basis_z, spectral, precision=precise)
    return spectral

def fractional(sat_vals, oil_coef):
    water_mob = sat_vals * sat_vals
    divisor = water_mob + oil_coef * (1.0 - sat_vals) * (1.0 - sat_vals)
    return (water_mob / divisor, 2.0 * oil_coef * sat_vals * (1.0 - sat_vals) / (divisor * divisor))

def neighbour(field_vals, along, offset):
    if along < 2:
        return jnp.roll(field_vals, -offset, along)
    zero_plane = jnp.zeros_like(field_vals[:, :, :1])
    if offset == 1:
        return jnp.concatenate([field_vals[:, :, 1:], zero_plane], axis=2)
    return jnp.concatenate([zero_plane, field_vals[:, :, :-1]], axis=2)

def harmonic(lower_mob, upper_mob):
    return 2.0 * lower_mob * upper_mob / (lower_mob + upper_mob)

def transmissibility(mobility):
    trans_x = harmonic(mobility, neighbour(mobility, 0, 1))
    trans_y = harmonic(mobility, neighbour(mobility, 1, 1))
    inner_z = harmonic(mobility[:, :, :-1], mobility[:, :, 1:])
    trans_z = jnp.concatenate([inner_z, jnp.zeros_like(mobility[:, :, :1])], axis=2)
    return (trans_x, trans_y, trans_z)

def face_of(face_arr, along, offset):
    if offset == 1:
        return face_arr
    return neighbour(face_arr, along, -1)

def operate(field_vals, trans_all, diag_coef):
    result = diag_coef * field_vals
    for along in range(3):
        for offset in (1, -1):
            result = result + face_of(trans_all[along], along, offset) * (field_vals - neighbour(field_vals, along, offset))
    return result

def precondition(residual, mobility):
    padded = jnp.pad(residual, ((INTERSECTION, INTERSECTION), (INTERSECTION, INTERSECTION), (0, 0)), mode='wrap')
    padded = jnp.pad(padded, ((0, 0), (0, 0), (INTERSECTION, INTERSECTION)))
    brick_count = N_GX * N_GY * N_GZ

    def one_brick(brick_id):
        index_x = brick_id // (N_GY * N_GZ)
        index_y = brick_id // N_GZ % N_GY
        index_z = brick_id % N_GZ
        starts = (index_x * CX, index_y * CY, index_z * CZ)
        box_field = lax.dynamic_slice(padded, starts, (CX + 2 * INTERSECTION, CY + 2 * INTERSECTION, CZ + 2 * INTERSECTION))
        local_mob = lax.dynamic_slice(mobility, starts, (CX, CY, CZ))
        solved = solve_box(box_field)
        return solved[INTERSECTION:INTERSECTION + CX, INTERSECTION:INTERSECTION + CY, INTERSECTION:INTERSECTION + CZ] / jnp.mean(local_mob)
    blocks = lax.map(one_brick, jnp.arange(brick_count, dtype=jnp.int32))
    blocks = blocks.reshape(N_GX, N_GY, N_GZ, CX, CY, CZ).transpose(0, 3, 1, 4, 2, 5)
    return blocks.reshape(NX, NY, NZ)

def reference(pressure, source, saturation, permeability, compress, porosity, rock_type, well_mask, oil_factor):
    oil_coef = oil_factor[rock_type]
    mobility = permeability * (saturation * saturation + oil_coef * (1.0 - saturation) * (1.0 - saturation))
    well_flag = well_mask.astype(jnp.float32)
    trans_all = transmissibility(mobility)
    diag_coef = compress + WELL_INDEX * well_flag * mobility
    residual = source - operate(pressure, trans_all, diag_coef)
    direction = precondition(residual, mobility)
    image_vec = operate(direction, trans_all, diag_coef)
    step_len = jnp.sum(residual * direction) / jnp.sum(direction * image_vec)
    pressure_new = pressure + step_len * direction
    residual_new = residual - step_len * image_vec
    storage_rate = porosity / TIME_STEP
    inject = INJECT_RATE * well_flag
    current = saturation
    for sweep_index in range(NEWTON):
        flow_frac, slope_val = fractional(current, oil_coef)
        balance = storage_rate * (current - saturation) - inject
        outflow = jnp.zeros_like(current)
        for along in range(3):
            for offset in (1, -1):
                face_flux = face_of(trans_all[along], along, offset) * (pressure_new - neighbour(pressure_new, along, offset))
                balance = balance + jnp.maximum(face_flux, 0.0) * flow_frac + jnp.minimum(face_flux, 0.0) * neighbour(flow_frac, along, offset)
                outflow = outflow + jnp.maximum(face_flux, 0.0)
        current = current - balance / (storage_rate + outflow * jnp.abs(slope_val))
    return (pressure_new, residual_new, current)
```

```python
import functools
import math

import jax
import jax.numpy as jnp
import ml_dtypes
import numpy as np
from jax import lax
from jax.experimental import pallas as pl
from jax.experimental.pallas import tpu as pltpu
from jax.sharding import PartitionSpec as P

MESH = pl.DeviceIdType.MESH
F32 = jnp.float32
BF16 = jnp.bfloat16

CX, CY, CZ = 32, 32, 128
W = 8
BX, BY, BZ = CX + 2 * W, CY + 2 * W, CZ + 2 * W
HALF = BX // 2
KEPT = CX // 2
CPAD = 256
NEWTON = 3
WELL_INDEX = 4.0
INJECT_RATE = 2.0
TIME_STEP = 0.05


def sine_basis(length):
    points = np.arange(length, dtype=np.float64) + 1.0
    table = math.sqrt(2.0 / (length + 1)) * np.sin(
        np.outer(points, points) * (math.pi / (length + 1))
    )
    return table, 2.0 - 2.0 * np.cos(points * (math.pi / (length + 1)))


def halves(table):
    high = table.astype(np.float32).astype(ml_dtypes.bfloat16)
    low = (table - high.astype(np.float64)).astype(np.float32).astype(ml_dtypes.bfloat16)
    return high, low


def stacked(table):
    return np.concatenate(halves(table), axis=0)


@functools.cache
def tables():
    sx, ex = sine_basis(BX)
    sy, ey = sine_basis(BY)
    sz, ez = sine_basis(BZ)
    zh, zl = (np.zeros((BZ, CPAD), ml_dtypes.bfloat16) for _ in range(2))
    zh[:, :BZ], zl[:, :BZ] = halves(sz)
    wz1 = np.concatenate([zh[W:-W], zh[W:-W]], axis=0)
    wz2 = np.zeros((2, 2 * CZ, CPAD), ml_dtypes.bfloat16)
    for layer, rows in ((0, slice(BZ - W, BZ)), (1, slice(0, W))):
        wz2[layer, :CZ] = zl[W:-W]
        wz2[layer, CZ : CZ + W] = zh[rows]
        wz2[layer, CZ + W : CZ + 2 * W] = zh[rows]
        wz2[layer, CZ + 2 * W : CZ + 3 * W] = zl[rows]
    eye8, eye4 = np.eye(8), np.eye(4)
    cx = np.stack([stacked(np.kron(sx[parity::2, :HALF], eye8)) for parity in range(2)])
    cxb = np.stack([stacked(np.kron(sx[W:HALF, parity::2], eye8)) for parity in range(2)])
    cy = stacked(np.kron(eye4, sy))
    cyb = stacked(np.kron(eye4, sy[W:-W]))
    wzb = np.zeros((2, CPAD, CZ), ml_dtypes.bfloat16)
    wzb[0, :BZ], wzb[1, :BZ] = halves(sz[:, W:-W])
    inv = np.zeros((2, HALF, BY, CPAD), np.float32)
    for parity in range(2):
        inv[parity, :, :, :BZ] = 1.0 / (
            ex[parity::2][:, None, None] + ey[None, :, None] + ez[None, None, :]
        )
    return wz1, wz2, cx, cy, cyb, cxb, wzb, inv


def split(value):
    high = value.astype(BF16)
    low = (value - high.astype(F32)).astype(BF16)
    return high, low


def mm(left, right):
    return jnp.dot(left, right, preferred_element_type=F32)


def mm_const(const, rows, value):
    high, low = split(value)
    both = mm(const, high)
    return both[:rows] + both[rows:] + mm(const[:rows], low)


def sweep(body, init, count=CX, unroll=2):
    return lax.fori_loop(0, count, body, init, unroll=unroll)


def kernel(sizes, *refs):
    n_gx, n_gy, n_gz = sizes
    (
        pressure, source, saturation, permeability, compress, porosity, rock, well, oil_factor,
        wz1_in, wz2_in, cx_in, cy_in, cyb_in, cxb_in, wzb_in, inv_in,
        pressure_out, residual_out, saturation_out,
        press, src, sat, perm, comp, poro, rocks, wells,
        wz1, wz2, cx, cy, cyb, cxb, wzb, inv,
        mob, frac0, frac1, frac2, oil, direc, sat_b,
        trans_x, trans_y, trans_z, flux_x, flux_y, flux_z, dflux_x, dflux_y, dflux_z,
        outflow, image,
        send1, recv1, send3, recv3, send4, recv4, send5, recv5,
        box, rz_send, rz, rz_all, rxz,
        a_hi, a_lo, a_halo, z1, x1, y1, w1,
        ar_send1, ar_recv1, ar_send2, ar_recv2,
        in_sems, const_sems, out_sems, send_sems, recv_sems,
    ) = refs
    mx, my, layer = lax.axis_index("gx"), lax.axis_index("gy"), lax.axis_index("gz")
    gx_low, gx_high = lax.rem(mx + n_gx - 1, n_gx), lax.rem(mx + 1, n_gx)
    gy_low, gy_high = lax.rem(my + n_gy - 1, n_gy), lax.rem(my + 1, n_gy)
    gz_other = lax.rem(layer + 1, n_gz)
    to_x = ({"gx": gx_low}, {"gx": gx_high})
    to_y = ({"gy": gy_low}, {"gy": gy_high})
    to_z = {"gz": gz_other}

    group1 = [(dx, dz) for dz in range(n_gz) for dx in range(n_gx) if dx or dz]
    peers1 = [
        {"gx": lax.rem(mx + dx, n_gx), "gz": lax.rem(layer + dz, n_gz)} for dx, dz in group1
    ]
    peers2 = [{"gy": lax.rem(my + dy, n_gy)} for dy in range(1, n_gy)]
    barrier = pltpu.get_barrier_semaphore()
    for peer in peers1 + peers2:
        pl.semaphore_signal(barrier, inc=1, device_id=peer, device_id_type=MESH)

    inner = (pl.ds(1, CX), pl.ds(8, CY))
    loads = [
        pltpu.make_async_copy(a, b, in_sems.at[i])
        for i, (a, b) in enumerate(
            (
                (saturation, sat), (permeability, perm), (rock, rocks), (pressure, press.at[inner]),
                (source, src), (compress, comp), (well, wells), (porosity, poro),
            )
        )
    ]
    for copy in loads:
        copy.start()
    const_loads = [
        pltpu.make_async_copy(a, b, const_sems.at[i])
        for i, (a, b) in enumerate(
            (
                (wz1_in, wz1), (wz2_in, wz2), (cx_in, cx), (cy_in, cy), (cyb_in, cyb),
                (cxb_in, cxb), (wzb_in, wzb), (inv_in, inv),
            )
        )
    ]
    for copy in const_loads:
        copy.start()

    used = [0]

    def remote(source_ref, target_ref, device):
        index = used[0]
        used[0] += 1
        return pltpu.make_async_remote_copy(
            src_ref=source_ref,
            dst_ref=target_ref,
            send_sem=send_sems.at[index],
            recv_sem=recv_sems.at[index],
            device_id=device,
            device_id_type=MESH,
        )

    lane = lax.broadcasted_iota(jnp.int32, (CY, CZ), 1)
    cur_lane = jnp.where(layer == 1, CZ - 1, -1)
    nxt_lane = jnp.where(layer == 0, CZ - 1, -1)
    low_lane = jnp.where(layer == 0, 0, -1)

    def upper(value):
        return jnp.where(lane == cur_lane, 0.0, value)

    def lower(value):
        return jnp.where(lane == low_lane, 0.0, pltpu.roll(value, 1, 1))

    def z_pair(value, halo, x):
        halo = pltpu.roll(halo, CZ - 1 - x, 1)
        return (
            jnp.where(lane == cur_lane, halo, value),
            jnp.where(lane == nxt_lane, halo, pltpu.roll(value, CZ - 1, 1)),
        )

    def z_pack(packed, value, x):
        moved = pltpu.roll(value, x + 1 - layer, 1)
        return jnp.where(lane == x, moved, packed)

    def put_rows(buffer, field, value, x):
        buffer[2, pl.ds(field * CX + x, 1), :] = value[0:1]
        buffer[3, pl.ds(field * CX + x, 1), :] = value[CY - 1 : CY]

    def exchange(send, recv, fields, packed):
        for i, field in enumerate(fields):
            span = pl.ds(i * CX, CX)
            send[0, span, :] = field[1, 8 : 8 + CY, :]
            send[1, span, :] = field[CX, 8 : 8 + CY, :]
            send[4, span, :] = packed[i]
        copies = [
            remote(send.at[0], recv.at[1], to_x[0]),
            remote(send.at[1], recv.at[0], to_x[1]),
            remote(send.at[2], recv.at[3], to_y[0]),
            remote(send.at[3], recv.at[2], to_y[1]),
            remote(send.at[4], recv.at[4], to_z),
        ]
        for copy in copies:
            copy.start()
        return copies

    def unpack(recv, fields):
        for i, field in enumerate(fields):
            span = pl.ds(i * CX, CX)
            field[0, 8 : 8 + CY, :] = recv[0, span, :]
            field[CX + 1, 8 : 8 + CY, :] = recv[1, span, :]

    def unpack_rows(recv, i, field, x):
        field[x + 1, 7:8, :] = recv[2, pl.ds(i * CX + x, 1), :]
        field[x + 1, 8 + CY : 9 + CY, :] = recv[3, pl.ds(i * CX + x, 1), :]

    def mid(field, x):
        return field[x, 8 : 8 + CY, :]

    def fraction(sat_vals, oil_vals):
        water = sat_vals * sat_vals
        rest = 1.0 - sat_vals
        inverse = 1.0 / (water + oil_vals * rest * rest)
        return water * inverse, 2.0 * oil_vals * sat_vals * rest * inverse * inverse

    factor = [oil_factor[k] for k in range(8)]
    for copy in loads[:4]:
        copy.wait()
    zero = jnp.zeros((CY, CZ), F32)

    def stage_a(x, carry):
        total, pack_p, pack_m, pack_f = carry
        kind = rocks[x]
        bit0, bit1, bit2 = (kind & 1) == 1, (kind & 2) == 2, (kind & 4) == 4
        pairs = [jnp.where(bit0, factor[2 * k + 1], factor[2 * k]) for k in range(4)]
        oil_vals = jnp.where(
            bit2, jnp.where(bit1, pairs[3], pairs[2]), jnp.where(bit1, pairs[1], pairs[0])
        )
        s = sat[x]
        rest = 1.0 - s
        water = s * s
        total_mob = water + oil_vals * rest * rest
        m = perm[x] * total_mob
        f = water / total_mob
        p = mid(press, x + 1)
        oil[x] = oil_vals
        mob[x + 1, 8 : 8 + CY, :] = m
        frac0[x + 1, 8 : 8 + CY, :] = f
        for i, value in enumerate((p, m, f)):
            put_rows(send1, i, value, x)
        return total + m, z_pack(pack_p, p, x), z_pack(pack_m, m, x), z_pack(pack_f, f, x)

    total, *packed = sweep(stage_a, (zero, zero, zero, zero))
    mean = jnp.sum(jnp.sum(total, axis=0, keepdims=True), axis=1, keepdims=True) * (
        1.0 / (CX * CY * CZ)
    )
    inv_mean = 1.0 / mean

    pl.semaphore_wait(barrier, len(peers1) + len(peers2))
    fields1 = (press, mob, frac0)
    round1 = exchange(send1, recv1, fields1, packed)
    for copy in loads[4:]:
        copy.wait()
    for copy in round1:
        copy.wait()
    unpack(recv1, fields1)
    rz_send[...] = jnp.zeros_like(rz_send)

    def harmonic(a, b):
        return 2.0 * a * b / (a + b)

    def x_face(x):
        tx = harmonic(mid(mob, x), mid(mob, x + 1))
        fx = tx * (mid(press, x) - mid(press, x + 1))
        trans_x[x] = tx
        flux_x[x] = fx
        return fx

    def stage_b(x, before):
        for i, field in enumerate(fields1):
            unpack_rows(recv1, i, field, x)
        fx = x_face(x + 1)
        ty = harmonic(mob[x + 1, 0:40, :], mob[x + 1, 1:41, :])
        fy = ty * (press[x + 1, 0:40, :] - press[x + 1, 1:41, :])
        trans_y[x] = ty
        flux_y[x] = fy
        m = mid(mob, x + 1)
        p = mid(press, x + 1)
        tz = harmonic(*z_pair(m, recv1[4, CX : 2 * CX, :], x))
        p_cur, p_nxt = z_pair(p, recv1[4, 0:CX, :], x)
        fz = tz * (p_cur - p_nxt)
        trans_z[x] = tz
        flux_z[x] = fz
        well_flag = wells[x].astype(F32)
        diag = comp[x] + WELL_INDEX * well_flag * m
        comp[x] = diag
        result = diag * p + (fx - before)
        result = result + (fy[8:40] - flux_y[x, 7:39, :])
        result = result + (upper(fz) - lower(fz))
        r = src[x] - result
        big = x + W
        box[big, W : W + CY, :] = r
        group = big // 16
        place = (big % 16) * 8
        moved = pltpu.roll(r, lax.rem(place + 8 * (1 - layer), CZ), 1)
        kept = rz_send[group, W : W + CY, :]
        rz_send[group, W : W + CY, :] = jnp.where(
            (lane >= place) & (lane < place + 8), moved, kept
        )
        return fx

    sweep(stage_b, x_face(0))

    yspan = pl.ds(W, CY)
    xspan = pl.ds(W, CX)
    low_rows, high_rows = pl.ds(0, W), pl.ds(W + CY, W)
    first_rows, last_rows = pl.ds(W, W), pl.ds(CY, W)
    copy_z = remote(rz_send.at[:, yspan], rz.at[:, yspan], to_z)
    copy_x = [
        remote(box.at[first_rows, yspan], box.at[high_rows, yspan], to_x[0]),
        remote(box.at[last_rows, yspan], box.at[low_rows, yspan], to_x[1]),
    ]
    copy_y = [
        remote(box.at[xspan, first_rows], box.at[xspan, high_rows], to_y[0]),
        remote(box.at[xspan, last_rows], box.at[xspan, low_rows], to_y[1]),
    ]
    copy_xz = [
        remote(rz.at[0, yspan], rxz.at[1], to_x[0]),
        remote(rz.at[2, yspan], rxz.at[0], to_x[1]),
    ]
    copy_xy = [
        remote(box.at[rows, first_rows], box.at[rows, high_rows], to_y[0])
        for rows in (low_rows, high_rows)
    ] + [
        remote(box.at[rows, last_rows], box.at[rows, low_rows], to_y[1])
        for rows in (low_rows, high_rows)
    ]
    copy_yz = [
        remote(rz_all.at[:, first_rows], rz_all.at[:, high_rows], to_y[0]),
        remote(rz_all.at[:, last_rows], rz_all.at[:, low_rows], to_y[1]),
    ]
    for copy in (copy_z, *copy_x, *copy_y):
        copy.start()
    copy_z.wait()
    for copy in copy_xz:
        copy.start()
    for copy in copy_xz:
        copy.wait()
    own_left = lane < CZ // 2
    rz_all[0, W : W + CY, :] = jnp.where(own_left, rxz[0], rz[0, W : W + CY, :])
    rz_all[1, W : W + CY, :] = rz[1, W : W + CY, :]
    rz_all[2, W : W + CY, :] = jnp.where(own_left, rz[2, W : W + CY, :], rxz[1])
    for copy in copy_yz:
        copy.start()
    for copy in copy_x:
        copy.wait()
    for copy in copy_xy:
        copy.start()
    for copy in (*copy_y, *copy_yz, *copy_xy):
        copy.wait()
    for copy in const_loads:
        copy.wait()

    wide_lane = lax.broadcasted_iota(jnp.int32, (BY, CZ), 1)

    def fold(i, carry):
        j = BX - 1 - i
        v, w = box[i], box[j]
        hv = pltpu.roll(rz_all[i // 16], lax.rem(CZ - (i % 16) * 8, CZ), 1)
        hw = pltpu.roll(rz_all[j // 16], lax.rem(CZ - (j % 16) * 8, CZ), 1)
        for parity, (main, halo) in enumerate(((v + w, hv + hw), (v - w, hv - hw))):
            rows = pl.ds(pl.multiple_of((parity * HALF + i) * BY, 16), BY)
            high, low = split(main)
            a_hi[rows, :] = high
            a_lo[rows, :] = low
            halo_high = halo.astype(BF16).astype(F32)
            halo_low = halo - halo_high
            tile = jnp.where(
                wide_lane < 8,
                halo_high,
                jnp.where(
                    wide_lane < 16, pltpu.roll(halo_low, 8, 1), pltpu.roll(halo_high, 16, 1)
                ),
            )
            a_halo[rows, :] = tile.astype(BF16)
        return carry

    sweep(fold, 0, HALF)
    weights2 = wz2[layer]
    for chunk in range(6):
        rows = slice(chunk * 384, (chunk + 1) * 384)
        high = a_hi[rows]
        out = mm(jnp.concatenate([high, a_lo[rows]], axis=1), wz1[...]) + mm(
            jnp.concatenate([high, a_halo[rows]], axis=1), weights2
        )
        z1[chunk // 3, (chunk % 3) * 8 : (chunk % 3) * 8 + 8] = out.reshape(8, BY, CPAD)
    for parity in range(2):
        for block in range(BY // 8):
            rows = slice(block * 8, block * 8 + 8)
            value = z1[parity, :, rows, :].reshape(HALF * 8, CPAD)
            out = mm_const(cx[parity], HALF * 8, value)
            x1[parity, :, rows, :] = out.reshape(HALF, 8, CPAD)
    for parity in range(2):
        for block in range(HALF // 4):
            span = slice(block * 4, block * 4 + 4)
            value = x1[parity, span].reshape(4 * BY, CPAD)
            out = mm_const(cy[...], 4 * BY, value) * inv[parity, span].reshape(4 * BY, CPAD)
            out = mm_const(cyb[...], 4 * CY, out)
            y1[parity, span] = out.reshape(4, CY, CPAD)
    for parity in range(2):
        for block in range(CY // 8):
            rows = slice(block * 8, block * 8 + 8)
            value = y1[parity, :, rows, :].reshape(HALF * 8, CPAD)
            out = mm_const(cxb[parity], KEPT * 8, value)
            w1[parity, :, rows, :] = out.reshape(KEPT, 8, CPAD)
    for block in range(4):
        span = slice(block * 4, block * 4 + 4)
        sides = []
        for parity in range(2):
            high, low = split(w1[parity, span].reshape(4 * CY, CPAD))
            sides.append(mm(high, wzb[0]) + mm(low, wzb[0]) + mm(high, wzb[1]))
        plus = (sides[0] + sides[1]) * inv_mean
        minus = (sides[0] - sides[1]) * inv_mean
        for k in range(4):
            i = block * 4 + k
            direc[1 + i, 8 : 8 + CY, :] = plus[k * CY : (k + 1) * CY]
            direc[CX - i, 8 : 8 + CY, :] = minus[k * CY : (k + 1) * CY]

    def stage_c(x, carry):
        along, pack_d = carry
        d = mid(direc, x + 1)
        put_rows(send3, 0, d, x)
        return along + d * box[x + W, W : W + CY, :], z_pack(pack_d, d, x)

    along, pack_d = sweep(stage_c, (zero, zero))
    round3 = exchange(send3, recv3, (direc,), (pack_d,))
    for copy in round3:
        copy.wait()
    unpack(recv3, (direc,))

    def d_face(x):
        fx = trans_x[x] * (mid(direc, x) - mid(direc, x + 1))
        dflux_x[x] = fx
        return fx

    def stage_d(x, carry):
        before, curve = carry
        unpack_rows(recv3, 0, direc, x)
        fx = d_face(x + 1)
        fy = trans_y[x] * (direc[x + 1, 0:40, :] - direc[x + 1, 1:41, :])
        dflux_y[x] = fy
        d = mid(direc, x + 1)
        d_cur, d_nxt = z_pair(d, recv3[4], x)
        fz = trans_z[x] * (d_cur - d_nxt)
        dflux_z[x] = fz
        result = comp[x] * d + (fx - before)
        result = result + (fy[8:40] - dflux_y[x, 7:39, :])
        result = result + (upper(fz) - lower(fz))
        image[x] = result
        return fx, curve + d * result

    _, curve = sweep(stage_d, (d_face(0), zero))

    ar_send1[...] = jnp.concatenate(
        [
            jnp.broadcast_to(jnp.sum(value, axis=0, keepdims=True), (4, CZ))
            for value in (along, curve)
        ],
        axis=0,
    )
    for send, recv, peers in ((ar_send1, ar_recv1, peers1), (ar_send2, ar_recv2, peers2)):
        copies = [remote(send, recv.at[i], peer) for i, peer in enumerate(peers)]
        for copy in copies:
            copy.start()
        for copy in copies:
            copy.wait()
        result = send[...]
        for i in range(len(peers)):
            result = result + recv[i]
        if send is ar_send1:
            ar_send2[...] = result
    sums = jnp.sum(result, axis=1, keepdims=True)
    step = sums[0:1] / sums[4:5]

    def total_x(x):
        fx = flux_x[x] + step * dflux_x[x]
        flux_x[x] = fx
        return fx, upwind_x(frac0, fx, x)

    def upwind_x(frac, fx, x):
        return fx * jnp.where(fx > 0.0, mid(frac, x), mid(frac, x + 1))

    def balance_of(frac, recv, field, fx_flow, flow_before, x, sat_vals):
        fy_low, fy_high = flux_y[x, 7:39, :], flux_y[x, 8:40, :]
        f = mid(frac, x + 1)
        flow_low = fy_low * jnp.where(fy_low > 0.0, frac[x + 1, 7:39, :], f)
        flow_high = fy_high * jnp.where(fy_high > 0.0, f, frac[x + 1, 9:41, :])
        f_cur, f_nxt = z_pair(f, recv[4, field * CX : (field + 1) * CX, :], x)
        fz = flux_z[x]
        flow_z = fz * jnp.where(fz > 0.0, f_cur, f_nxt)
        balance = (fx_flow - flow_before) + (flow_high - flow_low)
        balance = balance + (upper(flow_z) - lower(flow_z))
        return balance - INJECT_RATE * wells[x].astype(F32)

    def update(balance, storage, out_vals, sat_vals, oil_vals):
        _, slope = fraction(sat_vals, oil_vals)
        return sat_vals - balance / (storage + out_vals * jnp.abs(slope))

    def stage_e(x, carry):
        fx_before, flow_before, pack_f = carry
        d = mid(direc, x + 1)
        press[x + 1, 8 : 8 + CY, :] = mid(press, x + 1) + step * d
        src[x] = box[x + W, W : W + CY, :] - step * image[x]
        fx, flow = total_x(x + 1)
        flux_y[x] = flux_y[x] + step * dflux_y[x]
        fz = flux_z[x] + step * dflux_z[x]
        flux_z[x] = fz
        out_vals = jnp.maximum(fx, 0.0) + jnp.maximum(-fx_before, 0.0)
        out_vals = out_vals + jnp.maximum(flux_y[x, 8:40, :], 0.0)
        out_vals = out_vals + jnp.maximum(-flux_y[x, 7:39, :], 0.0)
        out_vals = out_vals + jnp.maximum(upper(fz), 0.0) + jnp.maximum(-lower(fz), 0.0)
        outflow[x] = out_vals
        storage = poro[x] / TIME_STEP
        s = sat[x]
        balance = balance_of(frac0, recv1, 2, flow, flow_before, x, s)
        s_new = update(balance, storage, out_vals, s, oil[x])
        sat_b[x] = s_new
        f_new, _ = fraction(s_new, oil[x])
        frac1[x + 1, 8 : 8 + CY, :] = f_new
        put_rows(send4, 0, f_new, x)
        return fx, flow, z_pack(pack_f, f_new, x)

    fx, flow = total_x(0)
    _, _, pack_f = sweep(stage_e, (fx, flow, zero))
    round4 = exchange(send4, recv4, (frac1,), (pack_f,))
    stores = [
        pltpu.make_async_copy(press.at[inner], pressure_out, out_sems.at[0]),
        pltpu.make_async_copy(src, residual_out, out_sems.at[1]),
    ]
    for copy in stores:
        copy.start()
    for copy in round4:
        copy.wait()
    unpack(recv4, (frac1,))

    def later(frac, recv, last, x, carry):
        flow_before, pack_f = carry
        unpack_rows(recv, 0, frac, x)
        flow = upwind_x(frac, flux_x[x + 1], x + 1)
        storage = poro[x] / TIME_STEP
        s = sat_b[x]
        balance = balance_of(frac, recv, 0, flow, flow_before, x, s)
        balance = balance + storage * (s - sat[x])
        s_new = update(balance, storage, outflow[x], s, oil[x])
        sat_b[x] = s_new
        if not last:
            f_new, _ = fraction(s_new, oil[x])
            frac2[x + 1, 8 : 8 + CY, :] = f_new
            put_rows(send5, 0, f_new, x)
            pack_f = z_pack(pack_f, f_new, x)
        return flow, pack_f

    flow = upwind_x(frac1, flux_x[0], 0)
    _, pack_f = sweep(functools.partial(later, frac1, recv4, False), (flow, zero))
    round5 = exchange(send5, recv5, (frac2,), (pack_f,))
    for copy in round5:
        copy.wait()
    unpack(recv5, (frac2,))
    flow = upwind_x(frac2, flux_x[0], 0)
    sweep(functools.partial(later, frac2, recv5, True), (flow, zero))
    last_store = pltpu.make_async_copy(sat_b, saturation_out, out_sems.at[2])
    last_store.start()
    for copy in (*stores, last_store):
        copy.wait()


def per_device(sizes, *args):
    consts = tables()
    brick = pltpu.VMEM((CX, CY, CZ), F32)
    bricki = pltpu.VMEM((CX, CY, CZ), jnp.int32)
    padded = pltpu.VMEM((CX + 2, BY, CZ), F32)
    faces_x = pltpu.VMEM((CX + 1, CY, CZ), F32)
    faces_y = pltpu.VMEM((CX, 40, CZ), F32)

    def buffers(fields):
        return [pltpu.VMEM((5, fields * CX, CZ), F32)] * 2

    rows = 2 * HALF * BY
    n1 = sizes[0] * sizes[2] - 1
    n2 = sizes[1] - 1
    tile = pltpu.VMEM((8, CZ), F32)
    n_remote = 5 * 4 + 13 + n1 + n2
    scratch = (
        [padded, brick, brick, brick, brick, brick, bricki, bricki]
        + [pltpu.VMEM(c.shape, c.dtype) for c in consts]
        + [padded] * 4
        + [brick, padded, brick]
        + [faces_x, faces_y, brick] * 3
        + [brick] * 2
        + buffers(3)
        + buffers(1) * 3
        + [pltpu.VMEM((BX, BY, CZ), F32)]
        + [pltpu.VMEM((3, BY, CZ), F32)] * 3
        + [pltpu.VMEM((2, CY, CZ), F32)]
        + [pltpu.VMEM((rows, CZ), BF16)] * 3
        + [pltpu.VMEM((2, HALF, BY, CPAD), F32)] * 2
        + [pltpu.VMEM((2, HALF, CY, CPAD), F32), pltpu.VMEM((2, KEPT, CY, CPAD), F32)]
        + [tile, pltpu.VMEM((n1, 8, CZ), F32), tile, pltpu.VMEM((n2, 8, CZ), F32)]
        + [pltpu.SemaphoreType.DMA((8,)), pltpu.SemaphoreType.DMA((8,))]
        + [pltpu.SemaphoreType.DMA((3,))]
        + [pltpu.SemaphoreType.DMA((n_remote,))] * 2
    )
    anywhere = pl.BlockSpec(memory_space=pl.ANY)
    in_specs = [anywhere] * 8 + [pl.BlockSpec(memory_space=pltpu.SMEM)] + [anywhere] * len(consts)
    return pl.pallas_call(
        functools.partial(kernel, sizes),
        out_shape=[jax.ShapeDtypeStruct((CX, CY, CZ), F32)] * 3,
        in_specs=in_specs,
        out_specs=[anywhere] * 3,
        scratch_shapes=scratch,
        compiler_params=pltpu.CompilerParams(
            collective_id=0, has_side_effects=True, vmem_limit_bytes=60 * 1024 * 1024
        ),
    )(*args, *(jnp.asarray(c) for c in consts))


def solution(mesh):
    sizes = tuple(mesh.shape[axis] for axis in ("gx", "gy", "gz"))
    spec = P("gx", "gy", "gz")
    return jax.shard_map(
        functools.partial(per_device, sizes),
        mesh=mesh,
        in_specs=(spec,) * 8 + (P(),),
        out_specs=(spec,) * 3,
        check_vma=False,
    )
```

```python
import functools
import math

import jax
import jax.numpy as jnp
import ml_dtypes
import numpy as np
from jax import lax
from jax.experimental import pallas as pl
from jax.experimental.pallas import tpu as pltpu
from jax.sharding import PartitionSpec as P

MESH = pl.DeviceIdType.MESH
F32 = jnp.float32
BF16 = jnp.bfloat16

CX, CY, CZ = 32, 32, 128
W = 8
BX, BY, BZ = CX + 2 * W, CY + 2 * W, CZ + 2 * W
HALF = BX // 2
KEPT = CX // 2
CPAD = 256
NEWTON = 3
WELL_INDEX = 4.0
INJECT_RATE = 2.0
TIME_STEP = 0.05


def sine_basis(length):
    points = np.arange(length, dtype=np.float64) + 1.0
    table = math.sqrt(2.0 / (length + 1)) * np.sin(
        np.outer(points, points) * (math.pi / (length + 1))
    )
    return table, 2.0 - 2.0 * np.cos(points * (math.pi / (length + 1)))


def halves(table):
    high = table.astype(np.float32).astype(ml_dtypes.bfloat16)
    low = (table - high.astype(np.float64)).astype(np.float32).astype(ml_dtypes.bfloat16)
    return high, low


def stacked(table):
    return np.concatenate(halves(table), axis=0)


@functools.cache
def tables():
    sx, ex = sine_basis(BX)
    sy, ey = sine_basis(BY)
    sz, ez = sine_basis(BZ)
    zh, zl = (np.zeros((BZ, CPAD), ml_dtypes.bfloat16) for _ in range(2))
    zh[:, :BZ], zl[:, :BZ] = halves(sz)
    wz1 = np.concatenate([zh[W:-W], zh[W:-W]], axis=0)
    wz2 = np.zeros((2, 2 * CZ, CPAD), ml_dtypes.bfloat16)
    for layer, rows in ((0, slice(BZ - W, BZ)), (1, slice(0, W))):
        wz2[layer, :CZ] = zl[W:-W]
        wz2[layer, CZ : CZ + W] = zh[rows]
        wz2[layer, CZ + W : CZ + 2 * W] = zh[rows]
        wz2[layer, CZ + 2 * W : CZ + 3 * W] = zl[rows]
    eye8, eye4 = np.eye(8), np.eye(4)
    cx = np.stack([stacked(np.kron(sx[parity::2, :HALF], eye8)) for parity in range(2)])
    cxb = np.stack([stacked(np.kron(sx[W:HALF, parity::2], eye8)) for parity in range(2)])
    cy = stacked(np.kron(eye4, sy))
    cyb = stacked(np.kron(eye4, sy[W:-W]))
    wzb = np.zeros((2, CPAD, CZ), ml_dtypes.bfloat16)
    wzb[0, :BZ], wzb[1, :BZ] = halves(sz[:, W:-W])
    inv = np.zeros((2, HALF, BY, CPAD), np.float32)
    for parity in range(2):
        inv[parity, :, :, :BZ] = 1.0 / (
            ex[parity::2][:, None, None] + ey[None, :, None] + ez[None, None, :]
        )
    return wz1, wz2, cx, cy, cyb, cxb, wzb, inv


def split(value):
    high = value.astype(BF16)
    low = (value - high.astype(F32)).astype(BF16)
    return high, low


def mm(left, right):
    return jnp.dot(left, right, preferred_element_type=F32)


def mm_const(const, rows, value):
    high, low = split(value)
    both = mm(const, high)
    return both[:rows] + both[rows:] + mm(const[:rows], low)


def sweep(body, init, count=CX, unroll=2):
    return lax.fori_loop(0, count, body, init, unroll=unroll)


def kernel(sizes, *refs):
    n_gx, n_gy, n_gz = sizes
    (
        pressure, source, saturation, permeability, compress, porosity, rock, well, oil_factor,
        wz1_in, wz2_in, cx_in, cy_in, cyb_in, cxb_in, wzb_in, inv_in,
        pressure_out, residual_out, saturation_out,
        press, src, sat, perm, comp, poro, rocks, wells,
        wz1, wz2, cx, cy, cyb, cxb, wzb, inv,
        mob, frac0, frac1, frac2, oil, direc, sat_b,
        trans_x, trans_y, trans_z, flux_x, flux_y, flux_z, dflux_x, dflux_y, dflux_z,
        outflow, image,
        send1, recv1, send3, recv3, send4, recv4, send5, recv5,
        box, rz_send, rz, rz_all, rxz,
        a_hi, a_lo, a_halo, z1, x1, y1, w1,
        face_t, face_p, face_d, face_o, face_f,
        ar_send1, ar_recv1, ar_send2, ar_recv2,
        in_sems, const_sems, out_sems, send_sems, recv_sems,
    ) = refs
    mx, my, layer = lax.axis_index("gx"), lax.axis_index("gy"), lax.axis_index("gz")

    def device(dx, dy, dz):
        return {
            "gx": lax.rem(mx + n_gx + dx, n_gx),
            "gy": lax.rem(my + n_gy + dy, n_gy),
            "gz": lax.rem(layer + n_gz + dz, n_gz),
        }

    peers1 = [device(dx, 0, dz) for dz in range(n_gz) for dx in range(n_gx) if dx or dz]
    peers2 = [device(0, dy, 0) for dy in range(1, n_gy)]
    steps = (-1, 0, 1)
    diagonal = [device(dx, dy, dz) for dz in (0, 1) for dx in steps for dy in steps if dy and (dx or dz)]
    everyone = peers1 + peers2 + diagonal
    barrier = pltpu.get_barrier_semaphore()
    for peer in everyone:
        pl.semaphore_signal(barrier, inc=1, device_id=peer, device_id_type=MESH)

    inner = (pl.ds(1, CX), pl.ds(8, CY))
    loads = [
        pltpu.make_async_copy(a, b, in_sems.at[i])
        for i, (a, b) in enumerate(
            (
                (saturation, sat), (permeability, perm), (rock, rocks), (pressure, press.at[inner]),
                (source, src), (compress, comp), (well, wells), (porosity, poro),
            )
        )
    ]
    for copy in loads:
        copy.start()
    const_loads = [
        pltpu.make_async_copy(a, b, const_sems.at[i])
        for i, (a, b) in enumerate(
            (
                (wz1_in, wz1), (wz2_in, wz2), (cx_in, cx), (cy_in, cy), (cyb_in, cyb),
                (cxb_in, cxb), (wzb_in, wzb), (inv_in, inv),
            )
        )
    ]
    for copy in const_loads:
        copy.start()

    used = [0]

    def remote(source_ref, target_ref, target):
        index = used[0]
        used[0] += 1
        return pltpu.make_async_remote_copy(
            src_ref=source_ref,
            dst_ref=target_ref,
            send_sem=send_sems.at[index],
            recv_sem=recv_sems.at[index],
            device_id=target,
            device_id_type=MESH,
        )

    lane = lax.broadcasted_iota(jnp.int32, (CY, CZ), 1)
    row8 = lax.broadcasted_iota(jnp.int32, (8, CZ), 0)
    face_lane = jnp.where(layer == 0, CZ - 1, 0)
    zero = jnp.zeros((CY, CZ), F32)

    def z_pack(packed, value, x):
        return jnp.where(lane == x, pltpu.roll(value, x + 1 - layer, 1), packed)

    def put_rows(buffer, field, value, x):
        buffer[2, pl.ds(field * CX + x, 1), :] = value[0:1]
        buffer[3, pl.ds(field * CX + x, 1), :] = value[CY - 1 : CY]

    def exchange(send, recv, fields, packed):
        for i, field in enumerate(fields):
            span = pl.ds(i * CX, CX)
            send[0, span, :] = field[1, 8 : 8 + CY, :]
            send[1, span, :] = field[CX, 8 : 8 + CY, :]
            send[4, span, :] = packed[i]
        copies = [
            remote(send.at[2], recv.at[3], device(0, -1, 0)),
            remote(send.at[3], recv.at[2], device(0, 1, 0)),
            remote(send.at[0], recv.at[1], device(-1, 0, 0)),
            remote(send.at[1], recv.at[0], device(1, 0, 0)),
            remote(send.at[4], recv.at[4], device(0, 0, 1)),
        ]
        for copy in copies:
            copy.start()
        return copies

    def part(buffer, field):
        return [buffer[k, field * CX : (field + 1) * CX, :] for k in range(5)]

    def at_faces(faces, x):
        value = jnp.where(x == 0, faces[0], 0.0) + jnp.where(x == CX - 1, faces[1], 0.0)
        moved = pltpu.roll(faces[4], lax.rem(CZ - 1 - x + layer, CZ), 1)
        value = value + jnp.where(lane == face_lane, moved, 0.0)
        first = value[0:8] + jnp.where(row8 == 0, faces[2, pl.ds(x, 1), :], 0.0)
        last = value[CY - 8 : CY] + jnp.where(row8 == 7, faces[3, pl.ds(x, 1), :], 0.0)
        return jnp.concatenate([first, value[8 : CY - 8], last], axis=0)

    def mid(field, x):
        return field[x, 8 : 8 + CY, :]

    def fraction(sat_vals, oil_vals):
        water = sat_vals * sat_vals
        rest = 1.0 - sat_vals
        inverse = 1.0 / (water + oil_vals * rest * rest)
        return water * inverse, 2.0 * oil_vals * sat_vals * rest * inverse * inverse

    def upwind(flux, here, there):
        return flux * jnp.where(flux > 0.0, here, there)

    for field in (mob, press, direc, frac0, frac1, frac2):
        field[0] = jnp.zeros((BY, CZ), F32)
        field[CX + 1] = jnp.zeros((BY, CZ), F32)

    def clear(x, carry):
        for field in (mob, press, direc, frac0, frac1, frac2):
            field[x + 1, 0:8, :] = zero[0:8]
            field[x + 1, 8 + CY : BY, :] = zero[0:8]
        return carry

    sweep(clear, 0)
    rz_send[...] = jnp.zeros_like(rz_send)

    factor = [oil_factor[k] for k in range(8)]
    for copy in loads[:4]:
        copy.wait()

    def stage_a(x, carry):
        total, pack_p, pack_m, pack_f = carry
        kind = rocks[x]
        bit0, bit1, bit2 = (kind & 1) == 1, (kind & 2) == 2, (kind & 4) == 4
        pairs = [jnp.where(bit0, factor[2 * k + 1], factor[2 * k]) for k in range(4)]
        oil_vals = jnp.where(
            bit2, jnp.where(bit1, pairs[3], pairs[2]), jnp.where(bit1, pairs[1], pairs[0])
        )
        s = sat[x]
        rest = 1.0 - s
        water = s * s
        total_mob = water + oil_vals * rest * rest
        m = perm[x] * total_mob
        f = water / total_mob
        p = mid(press, x + 1)
        oil[x] = oil_vals
        mob[x + 1, 8 : 8 + CY, :] = m
        frac0[x + 1, 8 : 8 + CY, :] = f
        for i, value in enumerate((p, m, f)):
            put_rows(send1, i, value, x)
        return total + m, z_pack(pack_p, p, x), z_pack(pack_m, m, x), z_pack(pack_f, f, x)

    total, *packed = sweep(stage_a, (zero, zero, zero, zero))
    mean = jnp.sum(jnp.sum(total, axis=0, keepdims=True), axis=1, keepdims=True) * (
        1.0 / (CX * CY * CZ)
    )
    inv_mean = 1.0 / mean

    pl.semaphore_wait(barrier, len(everyone))
    round1 = exchange(send1, recv1, (press, mob, frac0), packed)
    for copy in loads[4:]:
        copy.wait()

    def harmonic(a, b):
        return 2.0 * a * b / (a + b)

    def x_face(x):
        tx = harmonic(mid(mob, x), mid(mob, x + 1))
        fx = tx * (mid(press, x) - mid(press, x + 1))
        trans_x[x] = tx
        flux_x[x] = fx
        return fx

    def stage_b(x, before):
        fx = x_face(x + 1)
        ty = harmonic(mob[x + 1, 0:40, :], mob[x + 1, 1:41, :])
        fy = ty * (press[x + 1, 0:40, :] - press[x + 1, 1:41, :])
        trans_y[x] = ty
        flux_y[x] = fy
        m = mid(mob, x + 1)
        p = mid(press, x + 1)
        tz = jnp.where(lane == CZ - 1, 0.0, harmonic(m, pltpu.roll(m, CZ - 1, 1)))
        fz = tz * (p - pltpu.roll(p, CZ - 1, 1))
        trans_z[x] = tz
        flux_z[x] = fz
        diag = comp[x] + WELL_INDEX * wells[x].astype(F32) * m
        comp[x] = diag
        result = diag * p + (fx - before)
        result = result + (fy[8:40] - flux_y[x, 7:39, :])
        result = result + (fz - pltpu.roll(fz, 1, 1))
        box[x + W, W : W + CY, :] = src[x] - result
        return fx

    sweep(stage_b, x_face(0))
    for copy in round1:
        copy.wait()
    for k in range(5):
        own_p, own_m = (send1[k, i * CX : (i + 1) * CX, :] for i in range(2))
        far_p, far_m = (recv1[k, i * CX : (i + 1) * CX, :] for i in range(2))
        tk = harmonic(own_m, far_m)
        if k == 4:
            tk = jnp.where(lane < CX, tk, 0.0)
        face_t[k] = tk
        face_p[k] = tk * (own_p - far_p)

    def stage_r(x, carry):
        big = x + W
        r = box[big, W : W + CY, :] - at_faces(face_p, x)
        box[big, W : W + CY, :] = r
        group = big // 16
        place = (big % 16) * 8
        moved = pltpu.roll(r, lax.rem(place + 8 * (1 - layer), CZ), 1)
        kept = rz_send[group, W : W + CY, :]
        rz_send[group, W : W + CY, :] = jnp.where(
            (lane >= place) & (lane < place + 8), moved, kept
        )
        return carry

    inside = pl.ds(W, CX)
    cut = {-1: (pl.ds(W, W), pl.ds(W + CX, W)), 0: (inside, inside), 1: (pl.ds(CX, W), pl.ds(0, W))}
    wide_copies, far_copies = [], []
    for dx in (-1, 1, 0):
        for dy in (0, -1, 1):
            (sx, tx), (sy, ty) = cut[dx], cut[dy]
            if dx or dy:
                wide_copies.append(remote(box.at[sx, sy], box.at[tx, ty], device(dx, dy, 0)))
            if dx:
                mine, theirs = (0, 1) if dx < 0 else (2, 0)
                source_ref, target_ref = rz_send.at[mine, sy], rxz.at[theirs, ty]
            else:
                source_ref, target_ref = rz_send.at[:, sy], rz.at[:, ty]
            far_copies.append(remote(source_ref, target_ref, device(dx, dy, 1)))
    for k in range(2):
        lax.fori_loop(24 * k, 24 * k + 8, stage_r, 0, unroll=2)
        for copy in wide_copies[3 * k : 3 * k + 3]:
            copy.start()
    lax.fori_loop(8, 24, stage_r, 0, unroll=2)
    for copy in wide_copies[6:] + far_copies:
        copy.start()
    for copy in wide_copies + far_copies:
        copy.wait()
    for copy in const_loads:
        copy.wait()

    own_left = lax.broadcasted_iota(jnp.int32, (BY, CZ), 1) < CZ // 2
    rz_all[0] = jnp.where(own_left, rxz[0], rz[0])
    rz_all[1] = rz[1]
    rz_all[2] = jnp.where(own_left, rz[2], rxz[1])
    wide_lane = lax.broadcasted_iota(jnp.int32, (BY, CZ), 1)

    def fold(i, carry):
        j = BX - 1 - i
        v, w = box[i], box[j]
        hv = pltpu.roll(rz_all[i // 16], lax.rem(CZ - (i % 16) * 8, CZ), 1)
        hw = pltpu.roll(rz_all[j // 16], lax.rem(CZ - (j % 16) * 8, CZ), 1)
        for parity, (main, halo) in enumerate(((v + w, hv + hw), (v - w, hv - hw))):
            rows = pl.ds(pl.multiple_of((parity * HALF + i) * BY, 16), BY)
            high, low = split(main)
            a_hi[rows, :] = high
            a_lo[rows, :] = low
            halo_high = halo.astype(BF16).astype(F32)
            halo_low = halo - halo_high
            tile = jnp.where(
                wide_lane < 8,
                halo_high,
                jnp.where(
                    wide_lane < 16, pltpu.roll(halo_low, 8, 1), pltpu.roll(halo_high, 16, 1)
                ),
            )
            a_halo[rows, :] = tile.astype(BF16)
        return carry

    sweep(fold, 0, HALF, 4)
    weights2 = wz2[layer]
    for chunk in range(6):
        rows = slice(chunk * 384, (chunk + 1) * 384)
        high = a_hi[rows]
        out = mm(jnp.concatenate([high, a_lo[rows]], axis=1), wz1[...]) + mm(
            jnp.concatenate([high, a_halo[rows]], axis=1), weights2
        )
        z1[chunk // 3, (chunk % 3) * 8 : (chunk % 3) * 8 + 8] = out.reshape(8, BY, CPAD)
    for parity in range(2):
        for block in range(BY // 8):
            rows = slice(block * 8, block * 8 + 8)
            value = z1[parity, :, rows, :].reshape(HALF * 8, CPAD)
            out = mm_const(cx[parity], HALF * 8, value)
            x1[parity, :, rows, :] = out.reshape(HALF, 8, CPAD)
    for parity in range(2):
        for block in range(HALF // 4):
            span = slice(block * 4, block * 4 + 4)
            value = x1[parity, span].reshape(4 * BY, CPAD)
            out = mm_const(cy[...], 4 * BY, value) * inv[parity, span].reshape(4 * BY, CPAD)
            z1[parity, span] = out.reshape(4, BY, CPAD)
    for parity in range(2):
        for block in range(HALF // 4):
            span = slice(block * 4, block * 4 + 4)
            out = mm_const(cyb[...], 4 * CY, z1[parity, span].reshape(4 * BY, CPAD))
            y1[parity, span] = out.reshape(4, CY, CPAD)
    for parity in range(2):
        for block in range(CY // 8):
            rows = slice(block * 8, block * 8 + 8)
            value = y1[parity, :, rows, :].reshape(HALF * 8, CPAD)
            out = mm_const(cxb[parity], KEPT * 8, value)
            w1[parity, :, rows, :] = out.reshape(KEPT, 8, CPAD)
    for block in range(4):
        span = slice(block * 4, block * 4 + 4)
        sides = []
        for parity in range(2):
            high, low = split(w1[parity, span].reshape(4 * CY, CPAD))
            sides.append(mm(high, wzb[0]) + mm(low, wzb[0]) + mm(high, wzb[1]))
        plus = (sides[0] + sides[1]) * inv_mean
        minus = (sides[0] - sides[1]) * inv_mean
        for k in range(4):
            i = block * 4 + k
            direc[1 + i, 8 : 8 + CY, :] = plus[k * CY : (k + 1) * CY]
            direc[CX - i, 8 : 8 + CY, :] = minus[k * CY : (k + 1) * CY]

    def stage_c(x, carry):
        along, pack_d = carry
        d = mid(direc, x + 1)
        put_rows(send3, 0, d, x)
        return along + d * box[x + W, W : W + CY, :], z_pack(pack_d, d, x)

    along, pack_d = sweep(stage_c, (zero, zero))
    round3 = exchange(send3, recv3, (direc,), (pack_d,))

    def d_face(x):
        fx = trans_x[x] * (mid(direc, x) - mid(direc, x + 1))
        dflux_x[x] = fx
        return fx

    def stage_d(x, carry):
        before, curve = carry
        fx = d_face(x + 1)
        fy = trans_y[x] * (direc[x + 1, 0:40, :] - direc[x + 1, 1:41, :])
        dflux_y[x] = fy
        d = mid(direc, x + 1)
        fz = trans_z[x] * (d - pltpu.roll(d, CZ - 1, 1))
        dflux_z[x] = fz
        result = comp[x] * d + (fx - before)
        result = result + (fy[8:40] - dflux_y[x, 7:39, :])
        result = result + (fz - pltpu.roll(fz, 1, 1))
        image[x] = result
        return fx, curve + d * result

    _, curve = sweep(stage_d, (d_face(0), zero))
    for copy in round3:
        copy.wait()
    for k in range(5):
        fd = face_t[k] * (send3[k] - recv3[k])
        face_d[k] = fd
        curve = curve + send3[k] * fd

    ar_send1[...] = jnp.concatenate(
        [
            jnp.broadcast_to(jnp.sum(value, axis=0, keepdims=True), (4, CZ))
            for value in (along, curve)
        ],
        axis=0,
    )

    def finish_image(x, carry):
        image[x] = image[x] + at_faces(face_d, x)
        return carry

    for send, recv, peers in ((ar_send1, ar_recv1, peers1), (ar_send2, ar_recv2, peers2)):
        copies = [remote(send, recv.at[i], peer) for i, peer in enumerate(peers)]
        for copy in copies:
            copy.start()
        if send is ar_send1:
            sweep(finish_image, 0)
        for copy in copies:
            copy.wait()
        result = send[...]
        for i in range(len(peers)):
            result = result + recv[i]
        if send is ar_send1:
            ar_send2[...] = result
    sums = jnp.sum(result, axis=1, keepdims=True)
    step = sums[0:1] / sums[4:5]

    own_f, far_f = part(send1, 2), part(recv1, 2)
    for k in range(5):
        flux = face_p[k] + step * face_d[k]
        face_p[k] = flux
        face_o[k] = jnp.maximum(flux, 0.0)
        face_f[k] = upwind(flux, own_f[k], far_f[k])

    def total_x(x):
        fx = flux_x[x] + step * dflux_x[x]
        flux_x[x] = fx
        return fx, upwind(fx, mid(frac0, x), mid(frac0, x + 1))

    def balance_of(frac, fx_flow, flow_before, x):
        f = mid(frac, x + 1)
        flow_low = upwind(flux_y[x, 7:39, :], frac[x + 1, 7:39, :], f)
        flow_high = upwind(flux_y[x, 8:40, :], f, frac[x + 1, 9:41, :])
        flow_z = upwind(flux_z[x], f, pltpu.roll(f, CZ - 1, 1))
        balance = (fx_flow - flow_before) + (flow_high - flow_low)
        balance = balance + (flow_z - pltpu.roll(flow_z, 1, 1))
        return balance - INJECT_RATE * wells[x].astype(F32)

    def inverse_of(storage, out_vals, sat_vals, oil_vals):
        _, slope = fraction(sat_vals, oil_vals)
        return 1.0 / (storage + out_vals * jnp.abs(slope))

    def stage_e(x, carry):
        fx_before, flow_before, pack_f = carry
        d = mid(direc, x + 1)
        press[x + 1, 8 : 8 + CY, :] = mid(press, x + 1) + step * d
        src[x] = box[x + W, W : W + CY, :] - step * image[x]
        fx, flow = total_x(x + 1)
        flux_y[x] = flux_y[x] + step * dflux_y[x]
        fz = flux_z[x] + step * dflux_z[x]
        flux_z[x] = fz
        out_vals = jnp.maximum(fx, 0.0) + jnp.maximum(-fx_before, 0.0)
        out_vals = out_vals + jnp.maximum(flux_y[x, 8:40, :], 0.0)
        out_vals = out_vals + jnp.maximum(-flux_y[x, 7:39, :], 0.0)
        out_vals = out_vals + jnp.maximum(fz, 0.0) + jnp.maximum(-pltpu.roll(fz, 1, 1), 0.0)
        out_vals = out_vals + at_faces(face_o, x)
        outflow[x] = out_vals
        s = sat[x]
        balance = balance_of(frac0, flow, flow_before, x) + at_faces(face_f, x)
        s_new = s - balance * inverse_of(poro[x] / TIME_STEP, out_vals, s, oil[x])
        sat_b[x] = s_new
        f_new, _ = fraction(s_new, oil[x])
        frac1[x + 1, 8 : 8 + CY, :] = f_new
        put_rows(send4, 0, f_new, x)
        return fx, flow, z_pack(pack_f, f_new, x)

    fx, flow = total_x(0)
    _, _, pack_f = sweep(stage_e, (fx, flow, zero))
    round4 = exchange(send4, recv4, (frac1,), (pack_f,))
    stores = [
        pltpu.make_async_copy(press.at[inner], pressure_out, out_sems.at[0]),
        pltpu.make_async_copy(src, residual_out, out_sems.at[1]),
    ]
    for copy in stores:
        copy.start()

    def within(frac, x, flow_before):
        flow = upwind(flux_x[x + 1], mid(frac, x + 1), mid(frac, x + 2))
        storage = poro[x] / TIME_STEP
        s = sat_b[x]
        balance = balance_of(frac, flow, flow_before, x) + storage * (s - sat[x])
        inverse = inverse_of(storage, outflow[x], s, oil[x])
        image[x] = inverse
        sat_b[x] = s - balance * inverse
        return flow

    def across(last, x, pack_f):
        s_new = sat_b[x] - at_faces(face_f, x) * image[x]
        sat_b[x] = s_new
        if last:
            return pack_f
        f_new, _ = fraction(s_new, oil[x])
        frac2[x + 1, 8 : 8 + CY, :] = f_new
        put_rows(send5, 0, f_new, x)
        return z_pack(pack_f, f_new, x)

    def later(frac, send, recv, copies, last):
        sweep(functools.partial(within, frac), zero)
        for copy in copies:
            copy.wait()
        for k in range(5):
            face_f[k] = upwind(face_p[k], send[k], recv[k])
        return sweep(functools.partial(across, last), zero)

    pack_f = later(frac1, send4, recv4, round4, False)
    round5 = exchange(send5, recv5, (frac2,), (pack_f,))
    later(frac2, send5, recv5, round5, True)
    last_store = pltpu.make_async_copy(sat_b, saturation_out, out_sems.at[2])
    last_store.start()
    for copy in (*stores, last_store):
        copy.wait()


def per_device(sizes, *args):
    consts = tables()
    brick = pltpu.VMEM((CX, CY, CZ), F32)
    bricki = pltpu.VMEM((CX, CY, CZ), jnp.int32)
    padded = pltpu.VMEM((CX + 2, BY, CZ), F32)
    faces_x = pltpu.VMEM((CX + 1, CY, CZ), F32)
    faces_y = pltpu.VMEM((CX, 40, CZ), F32)

    def buffers(fields):
        return [pltpu.VMEM((5, fields * CX, CZ), F32)] * 2

    rows = 2 * HALF * BY
    n1 = sizes[0] * sizes[2] - 1
    n2 = sizes[1] - 1
    tile = pltpu.VMEM((8, CZ), F32)
    n_remote = 5 * 4 + 17 + n1 + n2
    scratch = (
        [padded, brick, brick, brick, brick, brick, bricki, bricki]
        + [pltpu.VMEM(c.shape, c.dtype) for c in consts]
        + [padded] * 4
        + [brick, padded, brick]
        + [faces_x, faces_y, brick] * 3
        + [brick] * 2
        + buffers(3)
        + buffers(1) * 3
        + [pltpu.VMEM((BX, BY, CZ), F32)]
        + [pltpu.VMEM((3, BY, CZ), F32)] * 3
        + [pltpu.VMEM((2, BY, CZ), F32)]
        + [pltpu.VMEM((rows, CZ), BF16)] * 3
        + [pltpu.VMEM((2, HALF, BY, CPAD), F32)] * 2
        + [pltpu.VMEM((2, HALF, CY, CPAD), F32), pltpu.VMEM((2, KEPT, CY, CPAD), F32)]
        + [pltpu.VMEM((5, CY, CZ), F32)] * 5
        + [tile, pltpu.VMEM((n1, 8, CZ), F32), tile, pltpu.VMEM((n2, 8, CZ), F32)]
        + [pltpu.SemaphoreType.DMA((8,)), pltpu.SemaphoreType.DMA((8,))]
        + [pltpu.SemaphoreType.DMA((3,))]
        + [pltpu.SemaphoreType.DMA((n_remote,))] * 2
    )
    anywhere = pl.BlockSpec(memory_space=pl.ANY)
    in_specs = [anywhere] * 8 + [pl.BlockSpec(memory_space=pltpu.SMEM)] + [anywhere] * len(consts)
    return pl.pallas_call(
        functools.partial(kernel, sizes),
        out_shape=[jax.ShapeDtypeStruct((CX, CY, CZ), F32)] * 3,
        in_specs=in_specs,
        out_specs=[anywhere] * 3,
        scratch_shapes=scratch,
        compiler_params=pltpu.CompilerParams(
            collective_id=0, has_side_effects=True, vmem_limit_bytes=60 * 1024 * 1024
        ),
    )(*args, *(jnp.asarray(c) for c in consts))


def solution(mesh):
    sizes = tuple(mesh.shape[axis] for axis in ("gx", "gy", "gz"))
    spec = P("gx", "gy", "gz")
    return jax.shard_map(
        functools.partial(per_device, sizes),
        mesh=mesh,
        in_specs=(spec,) * 8 + (P(),),
        out_specs=(spec,) * 3,
        check_vma=False,
    )
```

```python
import functools
import math

import jax
import jax.numpy as jnp
import ml_dtypes
import numpy as np
from jax import lax
from jax.experimental import pallas as pl
from jax.experimental.pallas import tpu as pltpu
from jax.sharding import PartitionSpec as P

MESH = pl.DeviceIdType.MESH
F32 = jnp.float32
BF16 = jnp.bfloat16

CX, CY, CZ = 32, 32, 128
W = 8
BX, BY, BZ = CX + 2 * W, CY + 2 * W, CZ + 2 * W
HALF = BX // 2
KEPT = CX // 2
CPAD = 256
NEWTON = 3
WELL_INDEX = 4.0
INJECT_RATE = 2.0
TIME_STEP = 0.05


def sine_basis(length):
    points = np.arange(length, dtype=np.float64) + 1.0
    table = math.sqrt(2.0 / (length + 1)) * np.sin(
        np.outer(points, points) * (math.pi / (length + 1))
    )
    return table, 2.0 - 2.0 * np.cos(points * (math.pi / (length + 1)))


def halves(table):
    high = table.astype(np.float32).astype(ml_dtypes.bfloat16)
    low = (table - high.astype(np.float64)).astype(np.float32).astype(ml_dtypes.bfloat16)
    return high, low


def stacked(table):
    return np.concatenate(halves(table), axis=0)


@functools.cache
def tables():
    sx, ex = sine_basis(BX)
    sy, ey = sine_basis(BY)
    sz, ez = sine_basis(BZ)
    zh, zl = (np.zeros((BZ, CPAD), ml_dtypes.bfloat16) for _ in range(2))
    zh[:, :BZ], zl[:, :BZ] = halves(sz)
    wz1 = np.concatenate([zh[W:-W], zh[W:-W]], axis=0)
    wz2 = np.zeros((2, 2 * CZ, CPAD), ml_dtypes.bfloat16)
    for layer, rows in ((0, slice(BZ - W, BZ)), (1, slice(0, W))):
        wz2[layer, :CZ] = zl[W:-W]
        wz2[layer, CZ : CZ + W] = zh[rows]
        wz2[layer, CZ + W : CZ + 2 * W] = zh[rows]
        wz2[layer, CZ + 2 * W : CZ + 3 * W] = zl[rows]
    eye8, eye4 = np.eye(8), np.eye(4)
    cx = np.stack([stacked(np.kron(sx[parity::2, :HALF], eye8)) for parity in range(2)])
    cxb = np.stack([stacked(np.kron(sx[W:HALF, parity::2], eye8)) for parity in range(2)])
    cy = stacked(np.kron(eye4, sy))
    cyb = stacked(np.kron(eye4, sy[W:-W]))
    wzb = np.zeros((2, CPAD, CZ), ml_dtypes.bfloat16)
    wzb[0, :BZ], wzb[1, :BZ] = halves(sz[:, W:-W])
    inv = np.zeros((2, HALF, BY, CPAD), np.float32)
    for parity in range(2):
        inv[parity, :, :, :BZ] = 1.0 / (
            ex[parity::2][:, None, None] + ey[None, :, None] + ez[None, None, :]
        )
    return wz1, wz2, cx, cy, cyb, cxb, wzb, inv


def split(value):
    high = value.astype(BF16)
    low = (value - high.astype(F32)).astype(BF16)
    return high, low


def mm(left, right):
    return jnp.dot(left, right, preferred_element_type=F32)


def mm_const(const, rows, value):
    high, low = split(value)
    both = mm(const, high)
    return both[:rows] + both[rows:] + mm(const[:rows], low)


def sweep(body, init, count=CX, unroll=8):
    return lax.fori_loop(0, count, body, init, unroll=unroll)


def kernel(sizes, *refs):
    n_gx, n_gy, n_gz = sizes
    (
        pressure, source, saturation, permeability, compress, porosity, rock, well, oil_factor,
        wz1_in, wz2_in, cx_in, cy_in, cyb_in, cxb_in, wzb_in, inv_in,
        pressure_out, residual_out, saturation_out,
        press, src, sat, perm, comp, poro, rocks, wells,
        wz1, wz2, cx, cy, cyb, cxb, wzb, inv,
        mob, frac0, frac1, frac2, oil, direc, sat_b,
        trans_x, trans_y, trans_z, flux_x, flux_y, flux_z, dflux_x, dflux_y, dflux_z,
        outflow, image,
        send1, recv1, send3, recv3, send4, recv4, send5, recv5,
        box, rz_send, rz, rz_all, rxz,
        a_hi, a_lo, a_halo, z1, x1, y1, w1,
        face_t, face_p, face_d, face_o, face_f,
        ar_send1, ar_recv1, ar_send2, ar_recv2,
        in_sems, const_sems, out_sems, send_sems, recv_sems,
    ) = refs
    mx, my, layer = lax.axis_index("gx"), lax.axis_index("gy"), lax.axis_index("gz")

    def device(dx, dy, dz):
        return {
            "gx": lax.rem(mx + n_gx + dx, n_gx),
            "gy": lax.rem(my + n_gy + dy, n_gy),
            "gz": lax.rem(layer + n_gz + dz, n_gz),
        }

    peers1 = [device(dx, 0, dz) for dz in range(n_gz) for dx in range(n_gx) if dx or dz]
    peers2 = [device(0, dy, 0) for dy in range(1, n_gy)]
    steps = (-1, 0, 1)
    diagonal = [device(dx, dy, dz) for dz in (0, 1) for dx in steps for dy in steps if dy and (dx or dz)]
    everyone = peers1 + peers2 + diagonal
    barrier = pltpu.get_barrier_semaphore()
    for peer in everyone:
        pl.semaphore_signal(barrier, inc=1, device_id=peer, device_id_type=MESH)

    inner = (pl.ds(1, CX), pl.ds(8, CY))
    loads = [
        pltpu.make_async_copy(a, b, in_sems.at[i])
        for i, (a, b) in enumerate(
            (
                (saturation, sat), (permeability, perm), (rock, rocks), (pressure, press.at[inner]),
                (source, src), (compress, comp), (well, wells), (porosity, poro),
            )
        )
    ]
    for copy in loads:
        copy.start()
    const_loads = [
        pltpu.make_async_copy(a, b, const_sems.at[i])
        for i, (a, b) in enumerate(
            (
                (wz1_in, wz1), (wz2_in, wz2), (cx_in, cx), (cy_in, cy), (cyb_in, cyb),
                (cxb_in, cxb), (wzb_in, wzb), (inv_in, inv),
            )
        )
    ]
    for copy in const_loads:
        copy.start()

    used = [0]

    def remote(source_ref, target_ref, target):
        index = used[0]
        used[0] += 1
        return pltpu.make_async_remote_copy(
            src_ref=source_ref,
            dst_ref=target_ref,
            send_sem=send_sems.at[index],
            recv_sem=recv_sems.at[index],
            device_id=target,
            device_id_type=MESH,
        )

    lane = lax.broadcasted_iota(jnp.int32, (CY, CZ), 1)
    row8 = lax.broadcasted_iota(jnp.int32, (8, CZ), 0)
    face_lane = jnp.where(layer == 0, CZ - 1, 0)
    zero = jnp.zeros((CY, CZ), F32)

    def z_pack(packed, value, x):
        return jnp.where(lane == x, pltpu.roll(value, x + 1 - layer, 1), packed)

    def put_rows(buffer, field, value, x):
        buffer[2, pl.ds(field * CX + x, 1), :] = value[0:1]
        buffer[3, pl.ds(field * CX + x, 1), :] = value[CY - 1 : CY]

    def exchange(send, recv, fields, packed):
        for i, field in enumerate(fields):
            span = pl.ds(i * CX, CX)
            send[0, span, :] = field[1, 8 : 8 + CY, :]
            send[1, span, :] = field[CX, 8 : 8 + CY, :]
            send[4, span, :] = packed[i]
        copies = [
            remote(send.at[2], recv.at[3], device(0, -1, 0)),
            remote(send.at[3], recv.at[2], device(0, 1, 0)),
            remote(send.at[0], recv.at[1], device(-1, 0, 0)),
            remote(send.at[1], recv.at[0], device(1, 0, 0)),
            remote(send.at[4], recv.at[4], device(0, 0, 1)),
        ]
        for copy in copies:
            copy.start()
        return copies

    def part(buffer, field):
        return [buffer[k, field * CX : (field + 1) * CX, :] for k in range(5)]

    def at_faces(faces, x):
        value = jnp.where(x == 0, faces[0], 0.0) + jnp.where(x == CX - 1, faces[1], 0.0)
        moved = pltpu.roll(faces[4], lax.rem(CZ - 1 - x + layer, CZ), 1)
        value = value + jnp.where(lane == face_lane, moved, 0.0)
        first = value[0:8] + jnp.where(row8 == 0, faces[2, pl.ds(x, 1), :], 0.0)
        last = value[CY - 8 : CY] + jnp.where(row8 == 7, faces[3, pl.ds(x, 1), :], 0.0)
        return jnp.concatenate([first, value[8 : CY - 8], last], axis=0)

    def mid(field, x):
        return field[x, 8 : 8 + CY, :]

    def fraction(sat_vals, oil_vals):
        water = sat_vals * sat_vals
        rest = 1.0 - sat_vals
        inverse = 1.0 / (water + oil_vals * rest * rest)
        return water * inverse, 2.0 * oil_vals * sat_vals * rest * inverse * inverse

    def upwind(flux, here, there):
        return flux * jnp.where(flux > 0.0, here, there)

    for field in (mob, press, direc, frac0, frac1, frac2):
        field[0] = jnp.zeros((BY, CZ), F32)
        field[CX + 1] = jnp.zeros((BY, CZ), F32)

    def clear(x, carry):
        for field in (mob, press, direc, frac0, frac1, frac2):
            field[x + 1, 0:8, :] = zero[0:8]
            field[x + 1, 8 + CY : BY, :] = zero[0:8]
        return carry

    sweep(clear, 0)
    rz_send[...] = jnp.zeros_like(rz_send)

    factor = [oil_factor[k] for k in range(8)]
    for copy in loads[:4]:
        copy.wait()

    def stage_a(x, carry):
        total, pack_p, pack_m, pack_f = carry
        kind = rocks[x]
        bit0, bit1, bit2 = (kind & 1) == 1, (kind & 2) == 2, (kind & 4) == 4
        pairs = [jnp.where(bit0, factor[2 * k + 1], factor[2 * k]) for k in range(4)]
        oil_vals = jnp.where(
            bit2, jnp.where(bit1, pairs[3], pairs[2]), jnp.where(bit1, pairs[1], pairs[0])
        )
        s = sat[x]
        rest = 1.0 - s
        water = s * s
        total_mob = water + oil_vals * rest * rest
        m = perm[x] * total_mob
        f = water / total_mob
        p = mid(press, x + 1)
        oil[x] = oil_vals
        mob[x + 1, 8 : 8 + CY, :] = m
        frac0[x + 1, 8 : 8 + CY, :] = f
        for i, value in enumerate((p, m, f)):
            put_rows(send1, i, value, x)
        return total + m, z_pack(pack_p, p, x), z_pack(pack_m, m, x), z_pack(pack_f, f, x)

    total, *packed = sweep(stage_a, (zero, zero, zero, zero))
    mean = jnp.sum(jnp.sum(total, axis=0, keepdims=True), axis=1, keepdims=True) * (
        1.0 / (CX * CY * CZ)
    )
    inv_mean = 1.0 / mean

    pl.semaphore_wait(barrier, len(everyone))
    round1 = exchange(send1, recv1, (press, mob, frac0), packed)
    for copy in loads[4:]:
        copy.wait()

    def harmonic(a, b):
        return 2.0 * a * b / (a + b)

    def x_face(x):
        tx = harmonic(mid(mob, x), mid(mob, x + 1))
        fx = tx * (mid(press, x) - mid(press, x + 1))
        trans_x[x] = tx
        flux_x[x] = fx
        return fx

    def stage_b(x, before):
        fx = x_face(x + 1)
        ty = harmonic(mob[x + 1, 0:40, :], mob[x + 1, 1:41, :])
        fy = ty * (press[x + 1, 0:40, :] - press[x + 1, 1:41, :])
        trans_y[x] = ty
        flux_y[x] = fy
        m = mid(mob, x + 1)
        p = mid(press, x + 1)
        tz = jnp.where(lane == CZ - 1, 0.0, harmonic(m, pltpu.roll(m, CZ - 1, 1)))
        fz = tz * (p - pltpu.roll(p, CZ - 1, 1))
        trans_z[x] = tz
        flux_z[x] = fz
        diag = comp[x] + WELL_INDEX * wells[x].astype(F32) * m
        comp[x] = diag
        result = diag * p + (fx - before)
        result = result + (fy[8:40] - flux_y[x, 7:39, :])
        result = result + (fz - pltpu.roll(fz, 1, 1))
        box[x + W, W : W + CY, :] = src[x] - result
        return fx

    sweep(stage_b, x_face(0))
    for copy in round1:
        copy.wait()
    for k in range(5):
        own_p, own_m = (send1[k, i * CX : (i + 1) * CX, :] for i in range(2))
        far_p, far_m = (recv1[k, i * CX : (i + 1) * CX, :] for i in range(2))
        tk = harmonic(own_m, far_m)
        if k == 4:
            tk = jnp.where(lane < CX, tk, 0.0)
        face_t[k] = tk
        face_p[k] = tk * (own_p - far_p)

    def stage_r(x, carry):
        big = x + W
        r = box[big, W : W + CY, :] - at_faces(face_p, x)
        box[big, W : W + CY, :] = r
        group = big // 16
        place = (big % 16) * 8
        moved = pltpu.roll(r, lax.rem(place + 8 * (1 - layer), CZ), 1)
        kept = rz_send[group, W : W + CY, :]
        rz_send[group, W : W + CY, :] = jnp.where(
            (lane >= place) & (lane < place + 8), moved, kept
        )
        return carry

    inside = pl.ds(W, CX)
    cut = {-1: (pl.ds(W, W), pl.ds(W + CX, W)), 0: (inside, inside), 1: (pl.ds(CX, W), pl.ds(0, W))}
    wide_copies, far_copies = [], []
    for dx in (-1, 1, 0):
        for dy in (0, -1, 1):
            (sx, tx), (sy, ty) = cut[dx], cut[dy]
            if dx or dy:
                wide_copies.append(remote(box.at[sx, sy], box.at[tx, ty], device(dx, dy, 0)))
            if dx:
                mine, theirs = (0, 1) if dx < 0 else (2, 0)
                source_ref, target_ref = rz_send.at[mine, sy], rxz.at[theirs, ty]
            else:
                source_ref, target_ref = rz_send.at[:, sy], rz.at[:, ty]
            far_copies.append(remote(source_ref, target_ref, device(dx, dy, 1)))
    for k in range(2):
        lax.fori_loop(24 * k, 24 * k + 8, stage_r, 0, unroll=8)
        for copy in wide_copies[3 * k : 3 * k + 3]:
            copy.start()
    lax.fori_loop(8, 24, stage_r, 0, unroll=8)
    for copy in wide_copies[6:] + far_copies:
        copy.start()
    for copy in wide_copies + far_copies:
        copy.wait()
    for copy in const_loads:
        copy.wait()

    own_left = lax.broadcasted_iota(jnp.int32, (BY, CZ), 1) < CZ // 2
    rz_all[0] = jnp.where(own_left, rxz[0], rz[0])
    rz_all[1] = rz[1]
    rz_all[2] = jnp.where(own_left, rz[2], rxz[1])
    wide_lane = lax.broadcasted_iota(jnp.int32, (BY, CZ), 1)

    def fold(i, carry):
        j = BX - 1 - i
        v, w = box[i], box[j]
        hv = pltpu.roll(rz_all[i // 16], lax.rem(CZ - (i % 16) * 8, CZ), 1)
        hw = pltpu.roll(rz_all[j // 16], lax.rem(CZ - (j % 16) * 8, CZ), 1)
        for parity, (main, halo) in enumerate(((v + w, hv + hw), (v - w, hv - hw))):
            rows = pl.ds(pl.multiple_of((parity * HALF + i) * BY, 16), BY)
            high, low = split(main)
            a_hi[rows, :] = high
            a_lo[rows, :] = low
            halo_high = halo.astype(BF16).astype(F32)
            halo_low = halo - halo_high
            tile = jnp.where(
                wide_lane < 8,
                halo_high,
                jnp.where(
                    wide_lane < 16, pltpu.roll(halo_low, 8, 1), pltpu.roll(halo_high, 16, 1)
                ),
            )
            a_halo[rows, :] = tile.astype(BF16)
        return carry

    sweep(fold, 0, HALF, 4)
    weights2 = wz2[layer]
    for chunk in range(6):
        rows = slice(chunk * 384, (chunk + 1) * 384)
        high = a_hi[rows]
        out = mm(jnp.concatenate([high, a_lo[rows]], axis=1), wz1[...]) + mm(
            jnp.concatenate([high, a_halo[rows]], axis=1), weights2
        )
        z1[chunk // 3, (chunk % 3) * 8 : (chunk % 3) * 8 + 8] = out.reshape(8, BY, CPAD)
    for parity in range(2):
        for block in range(BY // 8):
            rows = slice(block * 8, block * 8 + 8)
            value = z1[parity, :, rows, :].reshape(HALF * 8, CPAD)
            out = mm_const(cx[parity], HALF * 8, value)
            x1[parity, :, rows, :] = out.reshape(HALF, 8, CPAD)
    for parity in range(2):
        for block in range(HALF // 4):
            span = slice(block * 4, block * 4 + 4)
            value = x1[parity, span].reshape(4 * BY, CPAD)
            out = mm_const(cy[...], 4 * BY, value) * inv[parity, span].reshape(4 * BY, CPAD)
            z1[parity, span] = out.reshape(4, BY, CPAD)
    for parity in range(2):
        for block in range(HALF // 4):
            span = slice(block * 4, block * 4 + 4)
            out = mm_const(cyb[...], 4 * CY, z1[parity, span].reshape(4 * BY, CPAD))
            y1[parity, span] = out.reshape(4, CY, CPAD)
    for parity in range(2):
        for block in range(CY // 8):
            rows = slice(block * 8, block * 8 + 8)
            value = y1[parity, :, rows, :].reshape(HALF * 8, CPAD)
            out = mm_const(cxb[parity], KEPT * 8, value)
            w1[parity, :, rows, :] = out.reshape(KEPT, 8, CPAD)
    for block in range(4):
        span = slice(block * 4, block * 4 + 4)
        sides = []
        for parity in range(2):
            high, low = split(w1[parity, span].reshape(4 * CY, CPAD))
            sides.append(mm(high, wzb[0]) + mm(low, wzb[0]) + mm(high, wzb[1]))
        plus = (sides[0] + sides[1]) * inv_mean
        minus = (sides[0] - sides[1]) * inv_mean
        for k in range(4):
            i = block * 4 + k
            direc[1 + i, 8 : 8 + CY, :] = plus[k * CY : (k + 1) * CY]
            direc[CX - i, 8 : 8 + CY, :] = minus[k * CY : (k + 1) * CY]

    def stage_c(x, carry):
        along, pack_d = carry
        d = mid(direc, x + 1)
        put_rows(send3, 0, d, x)
        return along + d * box[x + W, W : W + CY, :], z_pack(pack_d, d, x)

    along, pack_d = sweep(stage_c, (zero, zero))
    round3 = exchange(send3, recv3, (direc,), (pack_d,))

    def d_face(x):
        fx = trans_x[x] * (mid(direc, x) - mid(direc, x + 1))
        dflux_x[x] = fx
        return fx

    def stage_d(x, carry):
        before, curve = carry
        fx = d_face(x + 1)
        fy = trans_y[x] * (direc[x + 1, 0:40, :] - direc[x + 1, 1:41, :])
        dflux_y[x] = fy
        d = mid(direc, x + 1)
        fz = trans_z[x] * (d - pltpu.roll(d, CZ - 1, 1))
        dflux_z[x] = fz
        result = comp[x] * d + (fx - before)
        result = result + (fy[8:40] - dflux_y[x, 7:39, :])
        result = result + (fz - pltpu.roll(fz, 1, 1))
        image[x] = result
        return fx, curve + d * result

    _, curve = sweep(stage_d, (d_face(0), zero))
    for copy in round3:
        copy.wait()
    for k in range(5):
        fd = face_t[k] * (send3[k] - recv3[k])
        face_d[k] = fd
        curve = curve + send3[k] * fd

    ar_send1[...] = jnp.concatenate(
        [
            jnp.broadcast_to(jnp.sum(value, axis=0, keepdims=True), (4, CZ))
            for value in (along, curve)
        ],
        axis=0,
    )

    def finish_image(x, carry):
        image[x] = image[x] + at_faces(face_d, x)
        return carry

    for send, recv, peers in ((ar_send1, ar_recv2, peers2), (ar_send2, ar_recv1, peers1)):
        copies = [remote(send, recv.at[i], peer) for i, peer in enumerate(peers)]
        for copy in copies:
            copy.start()
        if send is ar_send1:
            sweep(finish_image, 0)
        for copy in copies:
            copy.wait()
        result = send[...]
        for i in range(len(peers)):
            result = result + recv[i]
        if send is ar_send1:
            ar_send2[...] = result
    sums = jnp.sum(result, axis=1, keepdims=True)
    step = sums[0:1] / sums[4:5]

    own_f, far_f = part(send1, 2), part(recv1, 2)
    for k in range(5):
        flux = face_p[k] + step * face_d[k]
        face_p[k] = flux
        face_o[k] = jnp.maximum(flux, 0.0)
        face_f[k] = upwind(flux, own_f[k], far_f[k])

    def total_x(x):
        fx = flux_x[x] + step * dflux_x[x]
        flux_x[x] = fx
        return fx, upwind(fx, mid(frac0, x), mid(frac0, x + 1))

    def balance_of(frac, fx_flow, flow_before, x):
        f = mid(frac, x + 1)
        flow_low = upwind(flux_y[x, 7:39, :], frac[x + 1, 7:39, :], f)
        flow_high = upwind(flux_y[x, 8:40, :], f, frac[x + 1, 9:41, :])
        flow_z = upwind(flux_z[x], f, pltpu.roll(f, CZ - 1, 1))
        balance = (fx_flow - flow_before) + (flow_high - flow_low)
        balance = balance + (flow_z - pltpu.roll(flow_z, 1, 1))
        return balance - INJECT_RATE * wells[x].astype(F32)

    def inverse_of(storage, out_vals, sat_vals, oil_vals):
        _, slope = fraction(sat_vals, oil_vals)
        return 1.0 / (storage + out_vals * jnp.abs(slope))

    def stage_e(x, carry):
        fx_before, flow_before, pack_f = carry
        d = mid(direc, x + 1)
        press[x + 1, 8 : 8 + CY, :] = mid(press, x + 1) + step * d
        src[x] = box[x + W, W : W + CY, :] - step * image[x]
        fx, flow = total_x(x + 1)
        flux_y[x] = flux_y[x] + step * dflux_y[x]
        fz = flux_z[x] + step * dflux_z[x]
        flux_z[x] = fz
        out_vals = jnp.maximum(fx, 0.0) + jnp.maximum(-fx_before, 0.0)
        out_vals = out_vals + jnp.maximum(flux_y[x, 8:40, :], 0.0)
        out_vals = out_vals + jnp.maximum(-flux_y[x, 7:39, :], 0.0)
        out_vals = out_vals + jnp.maximum(fz, 0.0) + jnp.maximum(-pltpu.roll(fz, 1, 1), 0.0)
        out_vals = out_vals + at_faces(face_o, x)
        outflow[x] = out_vals
        s = sat[x]
        balance = balance_of(frac0, flow, flow_before, x) + at_faces(face_f, x)
        s_new = s - balance * inverse_of(poro[x] / TIME_STEP, out_vals, s, oil[x])
        sat_b[x] = s_new
        f_new, _ = fraction(s_new, oil[x])
        frac1[x + 1, 8 : 8 + CY, :] = f_new
        put_rows(send4, 0, f_new, x)
        return fx, flow, z_pack(pack_f, f_new, x)

    fx, flow = total_x(0)
    _, _, pack_f = sweep(stage_e, (fx, flow, zero))
    round4 = exchange(send4, recv4, (frac1,), (pack_f,))
    stores = [
        pltpu.make_async_copy(press.at[inner], pressure_out, out_sems.at[0]),
        pltpu.make_async_copy(src, residual_out, out_sems.at[1]),
    ]
    for copy in stores:
        copy.start()

    def within(frac, x, flow_before):
        flow = upwind(flux_x[x + 1], mid(frac, x + 1), mid(frac, x + 2))
        storage = poro[x] / TIME_STEP
        s = sat_b[x]
        balance = balance_of(frac, flow, flow_before, x) + storage * (s - sat[x])
        inverse = inverse_of(storage, outflow[x], s, oil[x])
        image[x] = inverse
        sat_b[x] = s - balance * inverse
        return flow

    def across(last, x, pack_f):
        s_new = sat_b[x] - at_faces(face_f, x) * image[x]
        sat_b[x] = s_new
        if last:
            return pack_f
        f_new, _ = fraction(s_new, oil[x])
        frac2[x + 1, 8 : 8 + CY, :] = f_new
        put_rows(send5, 0, f_new, x)
        return z_pack(pack_f, f_new, x)

    def later(frac, send, recv, copies, last):
        sweep(functools.partial(within, frac), zero)
        for copy in copies:
            copy.wait()
        for k in range(5):
            face_f[k] = upwind(face_p[k], send[k], recv[k])
        return sweep(functools.partial(across, last), zero)

    pack_f = later(frac1, send4, recv4, round4, False)
    round5 = exchange(send5, recv5, (frac2,), (pack_f,))
    later(frac2, send5, recv5, round5, True)
    last_store = pltpu.make_async_copy(sat_b, saturation_out, out_sems.at[2])
    last_store.start()
    for copy in (*stores, last_store):
        copy.wait()


def per_device(sizes, *args):
    consts = tables()
    brick = pltpu.VMEM((CX, CY, CZ), F32)
    bricki = pltpu.VMEM((CX, CY, CZ), jnp.int32)
    padded = pltpu.VMEM((CX + 2, BY, CZ), F32)
    faces_x = pltpu.VMEM((CX + 1, CY, CZ), F32)
    faces_y = pltpu.VMEM((CX, 40, CZ), F32)

    def buffers(fields):
        return [pltpu.VMEM((5, fields * CX, CZ), F32)] * 2

    rows = 2 * HALF * BY
    n1 = sizes[0] * sizes[2] - 1
    n2 = sizes[1] - 1
    tile = pltpu.VMEM((8, CZ), F32)
    n_remote = 5 * 4 + 17 + n1 + n2
    scratch = (
        [padded, brick, brick, brick, brick, brick, bricki, bricki]
        + [pltpu.VMEM(c.shape, c.dtype) for c in consts]
        + [padded] * 4
        + [brick, padded, brick]
        + [faces_x, faces_y, brick] * 3
        + [brick] * 2
        + buffers(3)
        + buffers(1) * 3
        + [pltpu.VMEM((BX, BY, CZ), F32)]
        + [pltpu.VMEM((3, BY, CZ), F32)] * 3
        + [pltpu.VMEM((2, BY, CZ), F32)]
        + [pltpu.VMEM((rows, CZ), BF16)] * 3
        + [pltpu.VMEM((2, HALF, BY, CPAD), F32)] * 2
        + [pltpu.VMEM((2, HALF, CY, CPAD), F32), pltpu.VMEM((2, KEPT, CY, CPAD), F32)]
        + [pltpu.VMEM((5, CY, CZ), F32)] * 5
        + [tile, pltpu.VMEM((n1, 8, CZ), F32), tile, pltpu.VMEM((n2, 8, CZ), F32)]
        + [pltpu.SemaphoreType.DMA((8,)), pltpu.SemaphoreType.DMA((8,))]
        + [pltpu.SemaphoreType.DMA((3,))]
        + [pltpu.SemaphoreType.DMA((n_remote,))] * 2
    )
    anywhere = pl.BlockSpec(memory_space=pl.ANY)
    in_specs = [anywhere] * 8 + [pl.BlockSpec(memory_space=pltpu.SMEM)] + [anywhere] * len(consts)
    results = pl.pallas_call(
        functools.partial(kernel, sizes),
        out_shape=[jax.ShapeDtypeStruct((CX, CY, CZ), F32)] * 3,
        in_specs=in_specs,
        out_specs=[anywhere] * 3,
        scratch_shapes=scratch,
        compiler_params=pltpu.CompilerParams(
            collective_id=0, has_side_effects=True, vmem_limit_bytes=60 * 1024 * 1024
        ),
    )(*args, *(jnp.asarray(c) for c in consts))

    whole = pl.BlockSpec((CX, CY, CZ), lambda: (0, 0, 0))
    return pl.pallas_call(
        handed_on,
        out_shape=[jax.ShapeDtypeStruct((CX, CY, CZ), F32)] * 3,
        in_specs=[whole] * 3,
        out_specs=[whole] * 3,
    )(*results)


def handed_on(*refs):
    for i in range(3):
        refs[3 + i][...] = refs[i][...]


def solution(mesh):
    sizes = tuple(mesh.shape[axis] for axis in ("gx", "gy", "gz"))
    spec = P("gx", "gy", "gz")
    return jax.shard_map(
        functools.partial(per_device, sizes),
        mesh=mesh,
        in_specs=(spec,) * 8 + (P(),),
        out_specs=(spec,) * 3,
        check_vma=False,
    )
```

```python
import functools
import math

import jax
import jax.numpy as jnp
import ml_dtypes
import numpy as np
from jax import lax
from jax.experimental import pallas as pl
from jax.experimental.pallas import tpu as pltpu
from jax.sharding import PartitionSpec as P

MESH = pl.DeviceIdType.MESH
F32 = jnp.float32
BF16 = jnp.bfloat16

CX, CY, CZ = 32, 32, 128
W = 8
BX, BY, BZ = CX + 2 * W, CY + 2 * W, CZ + 2 * W
HALF = BX // 2
KEPT = CX // 2
CPAD = 256
NEWTON = 3
WELL_INDEX = 4.0
INJECT_RATE = 2.0
TIME_STEP = 0.05


def sine_basis(length):
    points = np.arange(length, dtype=np.float64) + 1.0
    table = math.sqrt(2.0 / (length + 1)) * np.sin(
        np.outer(points, points) * (math.pi / (length + 1))
    )
    return table, 2.0 - 2.0 * np.cos(points * (math.pi / (length + 1)))


def halves(table):
    high = table.astype(np.float32).astype(ml_dtypes.bfloat16)
    low = (table - high.astype(np.float64)).astype(np.float32).astype(ml_dtypes.bfloat16)
    return high, low


def stacked(table):
    return np.concatenate(halves(table), axis=0)


@functools.cache
def tables():
    sx, ex = sine_basis(BX)
    sy, ey = sine_basis(BY)
    sz, ez = sine_basis(BZ)
    zh, zl = (np.zeros((BZ, CPAD), ml_dtypes.bfloat16) for _ in range(2))
    zh[:, :BZ], zl[:, :BZ] = halves(sz)
    wz1 = np.concatenate([zh[W:-W], zh[W:-W]], axis=0)
    wz2 = np.zeros((2, 2 * CZ, CPAD), ml_dtypes.bfloat16)
    for layer, rows in ((0, slice(BZ - W, BZ)), (1, slice(0, W))):
        wz2[layer, :CZ] = zl[W:-W]
        wz2[layer, CZ : CZ + W] = zh[rows]
        wz2[layer, CZ + W : CZ + 2 * W] = zh[rows]
        wz2[layer, CZ + 2 * W : CZ + 3 * W] = zl[rows]
    eye8, eye4 = np.eye(8), np.eye(4)
    cx = np.stack([stacked(np.kron(sx[parity::2, :HALF], eye8)) for parity in range(2)])
    cxb = np.stack([stacked(np.kron(sx[W:HALF, parity::2], eye8)) for parity in range(2)])
    cy = stacked(np.kron(eye4, sy))
    cyb = stacked(np.kron(eye4, sy[W:-W]))
    wzb = np.zeros((2, CPAD, CZ), ml_dtypes.bfloat16)
    wzb[0, :BZ], wzb[1, :BZ] = halves(sz[:, W:-W])
    inv = np.zeros((2, HALF, BY, CPAD), np.float32)
    for parity in range(2):
        inv[parity, :, :, :BZ] = 1.0 / (
            ex[parity::2][:, None, None] + ey[None, :, None] + ez[None, None, :]
        )
    return wz1, wz2, cx, cy, cyb, cxb, wzb, inv


def split(value):
    high = value.astype(BF16)
    low = (value - high.astype(F32)).astype(BF16)
    return high, low


def mm(left, right):
    return jnp.dot(left, right, preferred_element_type=F32)


def mm_const(const, rows, value):
    high, low = split(value)
    both = mm(const, high)
    return both[:rows] + both[rows:] + mm(const[:rows], low)


def sweep(body, init, count=CX, unroll=8):
    return lax.fori_loop(0, count, body, init, unroll=unroll)


def kernel(sizes, *refs):
    n_gx, n_gy, n_gz = sizes
    (
        pressure, source, saturation, permeability, compress, porosity, rock, well, oil_factor,
        wz1_in, wz2_in, cx_in, cy_in, cyb_in, cxb_in, wzb_in, inv_in,
        pressure_out, residual_out, saturation_out,
        press, src, sat, perm, comp, poro, rocks, wells,
        wz1, wz2, cx, cy, cyb, cxb, wzb, inv,
        mob, frac0, frac1, frac2, oil, direc, sat_b,
        trans_x, trans_y, trans_z, flux_x, flux_y, flux_z, dflux_x, dflux_y, dflux_z,
        outflow, image,
        send1, recv1, send3, recv3, send4, recv4, send5, recv5,
        box, rz_send, rz, rz_all, rxz,
        a_hi, a_lo, a_halo, z1, x1, y1, w1,
        face_t, face_p, face_d, face_o, face_f,
        ar_send1, ar_recv1, ar_send2, ar_recv2,
        in_sems, const_sems, out_sems, send_sems, recv_sems,
    ) = refs
    mx, my, layer = lax.axis_index("gx"), lax.axis_index("gy"), lax.axis_index("gz")

    def device(dx, dy, dz):
        moved = {}
        for axis, place, offset, size in (
            ("gx", mx, dx, n_gx), ("gy", my, dy, n_gy), ("gz", layer, dz, n_gz)
        ):
            if offset % size:
                moved[axis] = wrapped[axis, offset % size]
        return moved

    wrapped = {}
    for axis, place, size in (("gx", mx, n_gx), ("gy", my, n_gy), ("gz", layer, n_gz)):
        for offset in range(1, size):
            there = place + offset
            wrapped[axis, offset] = jnp.where(there >= size, there - size, there)

    peers1 = [device(dx, 0, dz) for dz in range(n_gz) for dx in range(n_gx) if dx or dz]
    peers2 = [device(0, dy, 0) for dy in range(1, n_gy)]
    steps = (-1, 0, 1)
    diagonal = [device(dx, dy, dz) for dz in (0, 1) for dx in steps for dy in steps if dy and (dx or dz)]
    everyone = peers1 + peers2 + diagonal
    barrier = pltpu.get_barrier_semaphore()
    for peer in everyone:
        pl.semaphore_signal(barrier, inc=1, device_id=peer, device_id_type=MESH)

    inner = (pl.ds(1, CX), pl.ds(8, CY))
    loads = [
        pltpu.make_async_copy(a, b, in_sems.at[i])
        for i, (a, b) in enumerate(
            (
                (saturation, sat), (permeability, perm), (rock, rocks), (pressure, press.at[inner]),
                (source, src), (compress, comp), (well, wells), (porosity, poro),
            )
        )
    ]
    for copy in loads:
        copy.start()
    const_loads = [
        pltpu.make_async_copy(a, b, const_sems.at[i])
        for i, (a, b) in enumerate(
            (
                (wz1_in, wz1), (wz2_in, wz2), (cx_in, cx), (cy_in, cy), (cyb_in, cyb),
                (cxb_in, cxb), (wzb_in, wzb), (inv_in, inv),
            )
        )
    ]
    for copy in const_loads:
        copy.start()

    used = [0]

    def remote(source_ref, target_ref, target):
        index = used[0]
        used[0] += 1
        return pltpu.make_async_remote_copy(
            src_ref=source_ref,
            dst_ref=target_ref,
            send_sem=send_sems.at[index],
            recv_sem=recv_sems.at[index],
            device_id=target,
            device_id_type=MESH,
        )

    lane = lax.broadcasted_iota(jnp.int32, (CY, CZ), 1)
    row8 = lax.broadcasted_iota(jnp.int32, (8, CZ), 0)
    face_lane = jnp.where(layer == 0, CZ - 1, 0)
    zero = jnp.zeros((CY, CZ), F32)

    def z_pack(packed, value, x):
        return jnp.where(lane == x, pltpu.roll(value, x + 1 - layer, 1), packed)

    def put_rows(buffer, field, value, x):
        buffer[2, pl.ds(field * CX + x, 1), :] = value[0:1]
        buffer[3, pl.ds(field * CX + x, 1), :] = value[CY - 1 : CY]

    def exchange(send, recv, fields, packed):
        for i, field in enumerate(fields):
            span = pl.ds(i * CX, CX)
            send[0, span, :] = field[1, 8 : 8 + CY, :]
            send[1, span, :] = field[CX, 8 : 8 + CY, :]
            send[4, span, :] = packed[i]
        copies = [
            remote(send.at[2], recv.at[3], device(0, -1, 0)),
            remote(send.at[3], recv.at[2], device(0, 1, 0)),
            remote(send.at[0], recv.at[1], device(-1, 0, 0)),
            remote(send.at[1], recv.at[0], device(1, 0, 0)),
            remote(send.at[4], recv.at[4], device(0, 0, 1)),
        ]
        for copy in copies:
            copy.start()
        return copies

    def part(buffer, field):
        return [buffer[k, field * CX : (field + 1) * CX, :] for k in range(5)]

    def at_faces(faces, x):
        value = jnp.where(x == 0, faces[0], 0.0) + jnp.where(x == CX - 1, faces[1], 0.0)
        moved = pltpu.roll(faces[4], lax.rem(CZ - 1 - x + layer, CZ), 1)
        value = value + jnp.where(lane == face_lane, moved, 0.0)
        first = value[0:8] + jnp.where(row8 == 0, faces[2, pl.ds(x, 1), :], 0.0)
        last = value[CY - 8 : CY] + jnp.where(row8 == 7, faces[3, pl.ds(x, 1), :], 0.0)
        return jnp.concatenate([first, value[8 : CY - 8], last], axis=0)

    def mid(field, x):
        return field[x, 8 : 8 + CY, :]

    def fraction(sat_vals, oil_vals):
        water = sat_vals * sat_vals
        rest = 1.0 - sat_vals
        inverse = 1.0 / (water + oil_vals * rest * rest)
        return water * inverse, 2.0 * oil_vals * sat_vals * rest * inverse * inverse

    def upwind(flux, here, there):
        return flux * jnp.where(flux > 0.0, here, there)

    for field in (mob, press, direc, frac0, frac1, frac2):
        field[0] = jnp.zeros((BY, CZ), F32)
        field[CX + 1] = jnp.zeros((BY, CZ), F32)

    def clear(x, carry):
        for field in (mob, press, direc, frac0, frac1, frac2):
            field[x + 1, 0:8, :] = zero[0:8]
            field[x + 1, 8 + CY : BY, :] = zero[0:8]
        return carry

    sweep(clear, 0)
    rz_send[...] = jnp.zeros_like(rz_send)

    factor = [oil_factor[k] for k in range(8)]
    for copy in loads[:4]:
        copy.wait()

    def stage_a(x, carry):
        total, pack_p, pack_m, pack_f = carry
        kind = rocks[x]
        bit0, bit1, bit2 = (kind & 1) == 1, (kind & 2) == 2, (kind & 4) == 4
        pairs = [jnp.where(bit0, factor[2 * k + 1], factor[2 * k]) for k in range(4)]
        oil_vals = jnp.where(
            bit2, jnp.where(bit1, pairs[3], pairs[2]), jnp.where(bit1, pairs[1], pairs[0])
        )
        s = sat[x]
        rest = 1.0 - s
        water = s * s
        total_mob = water + oil_vals * rest * rest
        m = perm[x] * total_mob
        f = water / total_mob
        p = mid(press, x + 1)
        oil[x] = oil_vals
        mob[x + 1, 8 : 8 + CY, :] = m
        frac0[x + 1, 8 : 8 + CY, :] = f
        for i, value in enumerate((p, m, f)):
            put_rows(send1, i, value, x)
        return total + m, z_pack(pack_p, p, x), z_pack(pack_m, m, x), z_pack(pack_f, f, x)

    total, *packed = sweep(stage_a, (zero, zero, zero, zero))
    mean = jnp.sum(jnp.sum(total, axis=0, keepdims=True), axis=1, keepdims=True) * (
        1.0 / (CX * CY * CZ)
    )
    inv_mean = 1.0 / mean

    pl.semaphore_wait(barrier, len(everyone))
    round1 = exchange(send1, recv1, (press, mob, frac0), packed)
    for copy in loads[4:]:
        copy.wait()

    def harmonic(a, b):
        return 2.0 * a * b / (a + b)

    def x_face(x):
        tx = harmonic(mid(mob, x), mid(mob, x + 1))
        fx = tx * (mid(press, x) - mid(press, x + 1))
        trans_x[x] = tx
        flux_x[x] = fx
        return fx

    def stage_b(x, before):
        fx = x_face(x + 1)
        ty = harmonic(mob[x + 1, 0:40, :], mob[x + 1, 1:41, :])
        fy = ty * (press[x + 1, 0:40, :] - press[x + 1, 1:41, :])
        trans_y[x] = ty
        flux_y[x] = fy
        m = mid(mob, x + 1)
        p = mid(press, x + 1)
        tz = jnp.where(lane == CZ - 1, 0.0, harmonic(m, pltpu.roll(m, CZ - 1, 1)))
        fz = tz * (p - pltpu.roll(p, CZ - 1, 1))
        trans_z[x] = tz
        flux_z[x] = fz
        diag = comp[x] + WELL_INDEX * wells[x].astype(F32) * m
        comp[x] = diag
        result = diag * p + (fx - before)
        result = result + (fy[8:40] - flux_y[x, 7:39, :])
        result = result + (fz - pltpu.roll(fz, 1, 1))
        box[x + W, W : W + CY, :] = src[x] - result
        return fx

    sweep(stage_b, x_face(0))
    for copy in round1:
        copy.wait()
    for k in range(5):
        own_p, own_m = (send1[k, i * CX : (i + 1) * CX, :] for i in range(2))
        far_p, far_m = (recv1[k, i * CX : (i + 1) * CX, :] for i in range(2))
        tk = harmonic(own_m, far_m)
        if k == 4:
            tk = jnp.where(lane < CX, tk, 0.0)
        face_t[k] = tk
        face_p[k] = tk * (own_p - far_p)

    def stage_r(x, carry):
        big = x + W
        r = box[big, W : W + CY, :] - at_faces(face_p, x)
        box[big, W : W + CY, :] = r
        group = big // 16
        place = (big % 16) * 8
        moved = pltpu.roll(r, lax.rem(place + 8 * (1 - layer), CZ), 1)
        kept = rz_send[group, W : W + CY, :]
        rz_send[group, W : W + CY, :] = jnp.where(
            (lane >= place) & (lane < place + 8), moved, kept
        )
        return carry

    inside = pl.ds(W, CX)
    cut = {-1: (pl.ds(W, W), pl.ds(W + CX, W)), 0: (inside, inside), 1: (pl.ds(CX, W), pl.ds(0, W))}
    wide_copies, far_copies = [], []
    for dx in (-1, 1, 0):
        for dy in (0, -1, 1):
            (sx, tx), (sy, ty) = cut[dx], cut[dy]
            if dx or dy:
                wide_copies.append(remote(box.at[sx, sy], box.at[tx, ty], device(dx, dy, 0)))
            if dx:
                mine, theirs = (0, 1) if dx < 0 else (2, 0)
                source_ref, target_ref = rz_send.at[mine, sy], rxz.at[theirs, ty]
            else:
                source_ref, target_ref = rz_send.at[:, sy], rz.at[:, ty]
            far_copies.append(remote(source_ref, target_ref, device(dx, dy, 1)))
    for k in range(2):
        lax.fori_loop(24 * k, 24 * k + 8, stage_r, 0, unroll=8)
        wide_copies[3 * k].start()
    lax.fori_loop(8, 24, stage_r, 0, unroll=8)
    for copy in far_copies[6:7] + wide_copies[6:] + far_copies[:6] + far_copies[7:] + wide_copies[1:3] + wide_copies[4:6]:
        copy.start()
    for copy in wide_copies:
        copy.wait()

    wide_lane = lax.broadcasted_iota(jnp.int32, (BY, CZ), 1)

    def fold(i, carry):
        j = BX - 1 - i
        v, w = box[i], box[j]
        for parity, main in enumerate((v + w, v - w)):
            rows = pl.ds(pl.multiple_of((parity * HALF + i) * BY, 16), BY)
            high, low = split(main)
            a_hi[rows, :] = high
            a_lo[rows, :] = low
        return carry

    sweep(fold, 0, HALF, 8)
    for copy in const_loads:
        copy.wait()
    weights2 = wz2[layer]
    for chunk in range(6):
        rows = slice(chunk * 384, (chunk + 1) * 384)
        high = a_hi[rows]
        out = mm(jnp.concatenate([high, a_lo[rows]], axis=1), wz1[...]) + mm(high, weights2[:CZ])
        z1[chunk // 3, (chunk % 3) * 8 : (chunk % 3) * 8 + 8] = out.reshape(8, BY, CPAD)
    for copy in far_copies:
        copy.wait()
    own_left = wide_lane < CZ // 2
    rz_all[0] = jnp.where(own_left, rxz[0], rz[0])
    rz_all[1] = rz[1]
    rz_all[2] = jnp.where(own_left, rz[2], rxz[1])

    def fold_far(i, carry):
        j = BX - 1 - i
        hv = pltpu.roll(rz_all[i // 16], lax.rem(CZ - (i % 16) * 8, CZ), 1)
        hw = pltpu.roll(rz_all[j // 16], lax.rem(CZ - (j % 16) * 8, CZ), 1)
        for parity, halo in enumerate((hv + hw, hv - hw)):
            rows = pl.ds(pl.multiple_of((parity * HALF + i) * BY, 16), BY)
            halo_high = halo.astype(BF16).astype(F32)
            halo_low = halo - halo_high
            tile = jnp.where(
                wide_lane < 8,
                halo_high,
                jnp.where(
                    wide_lane < 16, pltpu.roll(halo_low, 8, 1), pltpu.roll(halo_high, 16, 1)
                ),
            )
            a_halo[rows, :] = tile.astype(BF16)
        return carry

    sweep(fold_far, 0, HALF, 24)
    for chunk in range(6):
        rows = slice(chunk * 384, (chunk + 1) * 384)
        planes = slice((chunk % 3) * 8, (chunk % 3) * 8 + 8)
        out = mm(a_halo[rows], weights2[CZ:]).reshape(8, BY, CPAD)
        z1[chunk // 3, planes] = z1[chunk // 3, planes] + out
    for parity in range(2):
        for block in range(BY // 8):
            rows = slice(block * 8, block * 8 + 8)
            value = z1[parity, :, rows, :].reshape(HALF * 8, CPAD)
            out = mm_const(cx[parity], HALF * 8, value)
            x1[parity, :, rows, :] = out.reshape(HALF, 8, CPAD)
    for parity in range(2):
        for block in range(HALF // 4):
            span = slice(block * 4, block * 4 + 4)
            value = x1[parity, span].reshape(4 * BY, CPAD)
            out = mm_const(cy[...], 4 * BY, value) * inv[parity, span].reshape(4 * BY, CPAD)
            z1[parity, span] = out.reshape(4, BY, CPAD)
    for parity in range(2):
        for block in range(HALF // 4):
            span = slice(block * 4, block * 4 + 4)
            out = mm_const(cyb[...], 4 * CY, z1[parity, span].reshape(4 * BY, CPAD))
            y1[parity, span] = out.reshape(4, CY, CPAD)
    for parity in range(2):
        for block in range(CY // 8):
            rows = slice(block * 8, block * 8 + 8)
            value = y1[parity, :, rows, :].reshape(HALF * 8, CPAD)
            out = mm_const(cxb[parity], KEPT * 8, value)
            w1[parity, :, rows, :] = out.reshape(KEPT, 8, CPAD)
    for block in range(4):
        span = slice(block * 4, block * 4 + 4)
        sides = []
        for parity in range(2):
            high, low = split(w1[parity, span].reshape(4 * CY, CPAD))
            sides.append(mm(high, wzb[0]) + mm(low, wzb[0]) + mm(high, wzb[1]))
        plus = (sides[0] + sides[1]) * inv_mean
        minus = (sides[0] - sides[1]) * inv_mean
        for k in range(4):
            i = block * 4 + k
            direc[1 + i, 8 : 8 + CY, :] = plus[k * CY : (k + 1) * CY]
            direc[CX - i, 8 : 8 + CY, :] = minus[k * CY : (k + 1) * CY]

    def stage_c(x, carry):
        along, pack_d = carry
        d = mid(direc, x + 1)
        put_rows(send3, 0, d, x)
        return along + d * box[x + W, W : W + CY, :], z_pack(pack_d, d, x)

    along, pack_d = sweep(stage_c, (zero, zero), CX, 32)
    round3 = exchange(send3, recv3, (direc,), (pack_d,))

    def d_face(x):
        fx = trans_x[x] * (mid(direc, x) - mid(direc, x + 1))
        dflux_x[x] = fx
        return fx

    def stage_d(x, carry):
        before, curve = carry
        fx = d_face(x + 1)
        fy = trans_y[x] * (direc[x + 1, 0:40, :] - direc[x + 1, 1:41, :])
        dflux_y[x] = fy
        d = mid(direc, x + 1)
        fz = trans_z[x] * (d - pltpu.roll(d, CZ - 1, 1))
        dflux_z[x] = fz
        result = comp[x] * d + (fx - before)
        result = result + (fy[8:40] - dflux_y[x, 7:39, :])
        result = result + (fz - pltpu.roll(fz, 1, 1))
        image[x] = result
        return fx, curve + d * result

    _, curve = sweep(stage_d, (d_face(0), zero))
    for copy in round3:
        copy.wait()
    for k in range(5):
        fd = face_t[k] * (send3[k] - recv3[k])
        face_d[k] = fd
        curve = curve + send3[k] * fd

    ar_send1[...] = jnp.concatenate(
        [
            jnp.broadcast_to(jnp.sum(value, axis=0, keepdims=True), (4, CZ))
            for value in (along, curve)
        ],
        axis=0,
    )

    def finish_image(x, carry):
        image[x] = image[x] + at_faces(face_d, x)
        return carry

    def prepare(x, carry):
        poro[x] = poro[x] / TIME_STEP
        perm[x] = INJECT_RATE * wells[x].astype(F32)
        outflow[x] = jnp.abs(fraction(sat[x], oil[x])[1])
        return carry

    for send, recv, peers in ((ar_send1, ar_recv2, peers2), (ar_send2, ar_recv1, peers1)):
        copies = [remote(send, recv.at[i], peer) for i, peer in enumerate(peers)]
        for copy in copies:
            copy.start()
        sweep(finish_image if send is ar_send1 else prepare, 0)
        for copy in copies:
            copy.wait()
        result = send[...]
        for i in range(len(peers)):
            result = result + recv[i]
        if send is ar_send1:
            ar_send2[...] = result
    sums = jnp.sum(result, axis=1, keepdims=True)
    step = sums[0:1] / sums[4:5]

    own_f, far_f = part(send1, 2), part(recv1, 2)
    for k in range(5):
        flux = face_p[k] + step * face_d[k]
        face_p[k] = flux
        face_o[k] = jnp.maximum(flux, 0.0)
        face_f[k] = upwind(flux, own_f[k], far_f[k])

    def total_x(x):
        fx = flux_x[x] + step * dflux_x[x]
        flux_x[x] = fx
        return fx, upwind(fx, mid(frac0, x), mid(frac0, x + 1))

    def balance_of(frac, fx_flow, flow_before, x):
        f = mid(frac, x + 1)
        flow_low = upwind(flux_y[x, 7:39, :], frac[x + 1, 7:39, :], f)
        flow_high = upwind(flux_y[x, 8:40, :], f, frac[x + 1, 9:41, :])
        flow_z = upwind(flux_z[x], f, pltpu.roll(f, CZ - 1, 1))
        balance = (fx_flow - flow_before) + (flow_high - flow_low)
        balance = balance + (flow_z - pltpu.roll(flow_z, 1, 1))
        return balance - perm[x]

    def inverse_of(storage, out_vals, sat_vals, oil_vals):
        _, slope = fraction(sat_vals, oil_vals)
        return 1.0 / (storage + out_vals * jnp.abs(slope))

    def stage_e(x, carry):
        fx_before, flow_before, pack_f = carry
        d = mid(direc, x + 1)
        press[x + 1, 8 : 8 + CY, :] = mid(press, x + 1) + step * d
        src[x] = box[x + W, W : W + CY, :] - step * image[x]
        fx, flow = total_x(x + 1)
        flux_y[x] = flux_y[x] + step * dflux_y[x]
        fz = flux_z[x] + step * dflux_z[x]
        flux_z[x] = fz
        out_vals = jnp.maximum(fx, 0.0) + jnp.maximum(-fx_before, 0.0)
        out_vals = out_vals + jnp.maximum(flux_y[x, 8:40, :], 0.0)
        out_vals = out_vals + jnp.maximum(-flux_y[x, 7:39, :], 0.0)
        out_vals = out_vals + jnp.maximum(fz, 0.0) + jnp.maximum(-pltpu.roll(fz, 1, 1), 0.0)
        out_vals = out_vals + at_faces(face_o, x)
        slope = outflow[x]
        outflow[x] = out_vals
        s = sat[x]
        balance = balance_of(frac0, flow, flow_before, x) + at_faces(face_f, x)
        s_new = s - balance * (1.0 / (poro[x] + out_vals * slope))
        sat_b[x] = s_new
        f_new, _ = fraction(s_new, oil[x])
        frac1[x + 1, 8 : 8 + CY, :] = f_new
        put_rows(send4, 0, f_new, x)
        return fx, flow, z_pack(pack_f, f_new, x)

    fx, flow = total_x(0)
    _, _, pack_f = sweep(stage_e, (fx, flow, zero))
    round4 = exchange(send4, recv4, (frac1,), (pack_f,))
    stores = [
        pltpu.make_async_copy(press.at[inner], pressure_out, out_sems.at[0]),
        pltpu.make_async_copy(src, residual_out, out_sems.at[1]),
    ]
    for copy in stores:
        copy.start()

    def within(frac, x, flow_before):
        flow = upwind(flux_x[x + 1], mid(frac, x + 1), mid(frac, x + 2))
        storage = poro[x]
        s = sat_b[x]
        balance = balance_of(frac, flow, flow_before, x) + storage * (s - sat[x])
        inverse = inverse_of(storage, outflow[x], s, oil[x])
        image[x] = inverse
        sat_b[x] = s - balance * inverse
        return flow

    def across(last, x, pack_f):
        s_new = sat_b[x] - at_faces(face_f, x) * image[x]
        sat_b[x] = s_new
        if last:
            return pack_f
        f_new, _ = fraction(s_new, oil[x])
        frac2[x + 1, 8 : 8 + CY, :] = f_new
        put_rows(send5, 0, f_new, x)
        return z_pack(pack_f, f_new, x)

    def later(frac, send, recv, copies, last):
        sweep(functools.partial(within, frac), zero)
        for copy in copies:
            copy.wait()
        for k in range(5):
            face_f[k] = upwind(face_p[k], send[k], recv[k])
        return sweep(functools.partial(across, last), zero, CX, 16)

    pack_f = later(frac1, send4, recv4, round4, False)
    round5 = exchange(send5, recv5, (frac2,), (pack_f,))
    later(frac2, send5, recv5, round5, True)
    last_store = pltpu.make_async_copy(sat_b, saturation_out, out_sems.at[2])
    last_store.start()
    for copy in (*stores, last_store):
        copy.wait()


def per_device(sizes, *args):
    consts = tables()
    brick = pltpu.VMEM((CX, CY, CZ), F32)
    bricki = pltpu.VMEM((CX, CY, CZ), jnp.int32)
    padded = pltpu.VMEM((CX + 2, BY, CZ), F32)
    faces_x = pltpu.VMEM((CX + 1, CY, CZ), F32)
    faces_y = pltpu.VMEM((CX, 40, CZ), F32)

    def buffers(fields):
        return [pltpu.VMEM((5, fields * CX, CZ), F32)] * 2

    rows = 2 * HALF * BY
    n1 = sizes[0] * sizes[2] - 1
    n2 = sizes[1] - 1
    tile = pltpu.VMEM((8, CZ), F32)
    n_remote = 5 * 4 + 17 + n1 + n2
    scratch = (
        [padded, brick, brick, brick, brick, brick, bricki, bricki]
        + [pltpu.VMEM(c.shape, c.dtype) for c in consts]
        + [padded] * 4
        + [brick, padded, brick]
        + [faces_x, faces_y, brick] * 3
        + [brick] * 2
        + buffers(3)
        + buffers(1) * 3
        + [pltpu.VMEM((BX, BY, CZ), F32)]
        + [pltpu.VMEM((3, BY, CZ), F32)] * 3
        + [pltpu.VMEM((2, BY, CZ), F32)]
        + [pltpu.VMEM((rows, CZ), BF16)] * 3
        + [pltpu.VMEM((2, HALF, BY, CPAD), F32)] * 2
        + [pltpu.VMEM((2, HALF, CY, CPAD), F32), pltpu.VMEM((2, KEPT, CY, CPAD), F32)]
        + [pltpu.VMEM((5, CY, CZ), F32)] * 5
        + [tile, pltpu.VMEM((n1, 8, CZ), F32), tile, pltpu.VMEM((n2, 8, CZ), F32)]
        + [pltpu.SemaphoreType.DMA((8,)), pltpu.SemaphoreType.DMA((8,))]
        + [pltpu.SemaphoreType.DMA((3,))]
        + [pltpu.SemaphoreType.DMA((n_remote,))] * 2
    )
    anywhere = pl.BlockSpec(memory_space=pl.ANY)
    in_specs = [anywhere] * 8 + [pl.BlockSpec(memory_space=pltpu.SMEM)] + [anywhere] * len(consts)
    results = pl.pallas_call(
        functools.partial(kernel, sizes),
        out_shape=[jax.ShapeDtypeStruct((CX, CY, CZ), F32)] * 3,
        in_specs=in_specs,
        out_specs=[anywhere] * 3,
        scratch_shapes=scratch,
        compiler_params=pltpu.CompilerParams(
            collective_id=0, has_side_effects=True, vmem_limit_bytes=60 * 1024 * 1024
        ),
    )(*args, *(jnp.asarray(c) for c in consts))

    whole = pl.BlockSpec((CX, CY, CZ), lambda: (0, 0, 0))
    return pl.pallas_call(
        handed_on,
        out_shape=[jax.ShapeDtypeStruct((CX, CY, CZ), F32)] * 3,
        in_specs=[whole] * 3,
        out_specs=[whole] * 3,
    )(*results)


def handed_on(*refs):
    for i in range(3):
        refs[3 + i][...] = refs[i][...]


def solution(mesh):
    sizes = tuple(mesh.shape[axis] for axis in ("gx", "gy", "gz"))
    spec = P("gx", "gy", "gz")
    return jax.shard_map(
        functools.partial(per_device, sizes),
        mesh=mesh,
        in_specs=(spec,) * 8 + (P(),),
        out_specs=(spec,) * 3,
        check_vma=False,
    )
```

```python
import functools
import math

import jax
import jax.numpy as jnp
import ml_dtypes
import numpy as np
from jax import lax
from jax.experimental import pallas as pl
from jax.experimental.pallas import tpu as pltpu
from jax.sharding import PartitionSpec as P

MESH = pl.DeviceIdType.MESH
F32 = jnp.float32
BF16 = jnp.bfloat16

CX, CY, CZ = 32, 32, 128
W = 8
BX, BY, BZ = CX + 2 * W, CY + 2 * W, CZ + 2 * W
HALF = BX // 2
KEPT = CX // 2
CPAD = 256
NEWTON = 3
WELL_INDEX = 4.0
INJECT_RATE = 2.0
TIME_STEP = 0.05


def sine_basis(length):
    points = np.arange(length, dtype=np.float64) + 1.0
    table = math.sqrt(2.0 / (length + 1)) * np.sin(
        np.outer(points, points) * (math.pi / (length + 1))
    )
    return table, 2.0 - 2.0 * np.cos(points * (math.pi / (length + 1)))


def halves(table):
    high = table.astype(np.float32).astype(ml_dtypes.bfloat16)
    low = (table - high.astype(np.float64)).astype(np.float32).astype(ml_dtypes.bfloat16)
    return high, low


def stacked(table):
    return np.concatenate(halves(table), axis=0)


@functools.cache
def tables():
    sx, ex = sine_basis(BX)
    sy, ey = sine_basis(BY)
    sz, ez = sine_basis(BZ)
    zh, zl = (np.zeros((BZ, CPAD), ml_dtypes.bfloat16) for _ in range(2))
    zh[:, :BZ], zl[:, :BZ] = halves(sz)
    wz1 = np.concatenate([zh[W:-W], zh[W:-W]], axis=0)
    wz2 = np.zeros((2, 2 * CZ, CPAD), ml_dtypes.bfloat16)
    for layer, rows in ((0, slice(BZ - W, BZ)), (1, slice(0, W))):
        wz2[layer, :CZ] = zl[W:-W]
        wz2[layer, CZ : CZ + W] = zh[rows]
        wz2[layer, CZ + W : CZ + 2 * W] = zh[rows]
        wz2[layer, CZ + 2 * W : CZ + 3 * W] = zl[rows]
    eye8, eye4 = np.eye(8), np.eye(4)
    cx = np.stack([stacked(np.kron(sx[parity::2, :HALF], eye8)) for parity in range(2)])
    cxb = np.stack([stacked(np.kron(sx[W:HALF, parity::2], eye8)) for parity in range(2)])
    cy = stacked(np.kron(eye4, sy))
    cyb = stacked(np.kron(eye4, sy[W:-W]))
    wzb = np.zeros((2, CPAD, CZ), ml_dtypes.bfloat16)
    wzb[0, :BZ], wzb[1, :BZ] = halves(sz[:, W:-W])
    inv = np.zeros((2, HALF, BY, CPAD), np.float32)
    for parity in range(2):
        inv[parity, :, :, :BZ] = 1.0 / (
            ex[parity::2][:, None, None] + ey[None, :, None] + ez[None, None, :]
        )
    return wz1, wz2, cx, cy, cyb, cxb, wzb, inv


def split(value):
    high = value.astype(BF16)
    low = (value - high.astype(F32)).astype(BF16)
    return high, low


def mm(left, right):
    return jnp.dot(left, right, preferred_element_type=F32)


def mm_const(const, rows, value):
    high, low = split(value)
    both = mm(const, high)
    return both[:rows] + both[rows:] + mm(const[:rows], low)


def sweep(body, init, count=CX, unroll=8):
    return lax.fori_loop(0, count, body, init, unroll=unroll)


def kernel(sizes, *refs):
    n_gx, n_gy, n_gz = sizes
    (
        pressure, source, saturation, permeability, compress, porosity, rock, well, oil_factor,
        wz1_in, wz2_in, cx_in, cy_in, cyb_in, cxb_in, wzb_in, inv_in,
        pressure_out, residual_out, saturation_out,
        press, src, sat, perm, comp, poro, rocks, wells,
        wz1, wz2, cx, cy, cyb, cxb, wzb, inv,
        mob, frac0, frac1, frac2, oil, direc, sat_b,
        trans_x, trans_y, trans_z, flux_x, flux_y, flux_z, dflux_x, dflux_y, dflux_z,
        outflow, image,
        send1, recv1, send3, recv3, send4, recv4, send5, recv5,
        box, rz_send, rz, rz_all, rxz,
        a_hi, a_lo, a_halo, z1, x1, y1, w1,
        face_t, face_p, face_d, face_o, face_f,
        ar_send1, ar_recv1, ar_send2, ar_recv2,
        in_sems, const_sems, out_sems, send_sems, recv_sems,
    ) = refs
    mx, my, layer = lax.axis_index("gx"), lax.axis_index("gy"), lax.axis_index("gz")

    def device(dx, dy, dz):
        moved = {}
        for axis, place, offset, size in (
            ("gx", mx, dx, n_gx), ("gy", my, dy, n_gy), ("gz", layer, dz, n_gz)
        ):
            if offset % size:
                moved[axis] = wrapped[axis, offset % size]
        return moved

    wrapped = {}
    for axis, place, size in (("gx", mx, n_gx), ("gy", my, n_gy), ("gz", layer, n_gz)):
        for offset in range(1, size):
            there = place + offset
            wrapped[axis, offset] = jnp.where(there >= size, there - size, there)

    peers1 = [device(dx, 0, dz) for dz in range(n_gz) for dx in range(n_gx) if dx or dz]
    peers2 = [device(0, dy, 0) for dy in range(1, n_gy)]
    steps = (-1, 0, 1)
    diagonal = [device(dx, dy, dz) for dz in (0, 1) for dx in steps for dy in steps if dy and (dx or dz)]
    everyone = peers1 + peers2 + diagonal
    barrier = pltpu.get_barrier_semaphore()
    for peer in everyone:
        pl.semaphore_signal(barrier, inc=1, device_id=peer, device_id_type=MESH)

    inner = (pl.ds(1, CX), pl.ds(8, CY))
    loads = [
        pltpu.make_async_copy(a, b, in_sems.at[i])
        for i, (a, b) in enumerate(
            (
                (saturation, sat), (permeability, perm), (rock, rocks), (pressure, press.at[inner]),
                (source, src), (compress, comp), (well, wells), (porosity, poro),
            )
        )
    ]
    for copy in loads:
        copy.start()
    const_loads = [
        pltpu.make_async_copy(a, b, const_sems.at[i])
        for i, (a, b) in enumerate(
            (
                (wz1_in, wz1), (wz2_in, wz2), (cx_in, cx), (cy_in, cy), (cyb_in, cyb),
                (cxb_in, cxb), (wzb_in, wzb), (inv_in, inv),
            )
        )
    ]
    for copy in const_loads:
        copy.start()

    used = [0]

    def remote(source_ref, target_ref, target):
        index = used[0]
        used[0] += 1
        return pltpu.make_async_remote_copy(
            src_ref=source_ref,
            dst_ref=target_ref,
            send_sem=send_sems.at[index],
            recv_sem=recv_sems.at[index],
            device_id=target,
            device_id_type=MESH,
        )

    lane = lax.broadcasted_iota(jnp.int32, (CY, CZ), 1)
    row8 = lax.broadcasted_iota(jnp.int32, (8, CZ), 0)
    face_lane = jnp.where(layer == 0, CZ - 1, 0)
    zero = jnp.zeros((CY, CZ), F32)

    def z_pack(packed, value, x):
        return jnp.where(lane == x, pltpu.roll(value, x + 1 - layer, 1), packed)

    def put_rows(buffer, field, value, x):
        buffer[2, pl.ds(field * CX + x, 1), :] = value[0:1]
        buffer[3, pl.ds(field * CX + x, 1), :] = value[CY - 1 : CY]

    def exchange(send, recv, fields, packed):
        for i, field in enumerate(fields):
            span = pl.ds(i * CX, CX)
            send[0, span, :] = field[1, 8 : 8 + CY, :]
            send[1, span, :] = field[CX, 8 : 8 + CY, :]
            send[4, span, :] = packed[i]
        copies = [
            remote(send.at[2], recv.at[3], device(0, -1, 0)),
            remote(send.at[3], recv.at[2], device(0, 1, 0)),
            remote(send.at[0], recv.at[1], device(-1, 0, 0)),
            remote(send.at[1], recv.at[0], device(1, 0, 0)),
            remote(send.at[4], recv.at[4], device(0, 0, 1)),
        ]
        for copy in copies:
            copy.start()
        return copies

    def part(buffer, field):
        return [buffer[k, field * CX : (field + 1) * CX, :] for k in range(5)]

    def at_faces(faces, x):
        value = jnp.where(x == 0, faces[0], 0.0) + jnp.where(x == CX - 1, faces[1], 0.0)
        moved = pltpu.roll(faces[4], lax.rem(CZ - 1 - x + layer, CZ), 1)
        value = value + jnp.where(lane == face_lane, moved, 0.0)
        first = value[0:8] + jnp.where(row8 == 0, faces[2, pl.ds(x, 1), :], 0.0)
        last = value[CY - 8 : CY] + jnp.where(row8 == 7, faces[3, pl.ds(x, 1), :], 0.0)
        return jnp.concatenate([first, value[8 : CY - 8], last], axis=0)

    def mid(field, x):
        return field[x, 8 : 8 + CY, :]

    def fraction(sat_vals, oil_vals):
        water = sat_vals * sat_vals
        rest = 1.0 - sat_vals
        inverse = 1.0 / (water + oil_vals * rest * rest)
        return water * inverse, 2.0 * oil_vals * sat_vals * rest * inverse * inverse

    def upwind(flux, here, there):
        return flux * jnp.where(flux > 0.0, here, there)

    for field in (mob, press, direc, frac0, frac1, frac2):
        field[0] = jnp.zeros((BY, CZ), F32)
        field[CX + 1] = jnp.zeros((BY, CZ), F32)

    def clear(x, carry):
        for field in (mob, press, direc, frac0, frac1, frac2):
            field[x + 1, 0:8, :] = zero[0:8]
            field[x + 1, 8 + CY : BY, :] = zero[0:8]
        return carry

    sweep(clear, 0)
    rz_send[...] = jnp.zeros_like(rz_send)

    factor = [oil_factor[k] for k in range(8)]
    for copy in loads[:4]:
        copy.wait()

    def stage_a(x, carry):
        total, pack_p, pack_m, pack_f = carry
        kind = rocks[x]
        bit0, bit1, bit2 = (kind & 1) == 1, (kind & 2) == 2, (kind & 4) == 4
        pairs = [jnp.where(bit0, factor[2 * k + 1], factor[2 * k]) for k in range(4)]
        oil_vals = jnp.where(
            bit2, jnp.where(bit1, pairs[3], pairs[2]), jnp.where(bit1, pairs[1], pairs[0])
        )
        s = sat[x]
        rest = 1.0 - s
        water = s * s
        total_mob = water + oil_vals * rest * rest
        m = perm[x] * total_mob
        f = water / total_mob
        p = mid(press, x + 1)
        oil[x] = oil_vals
        mob[x + 1, 8 : 8 + CY, :] = m
        frac0[x + 1, 8 : 8 + CY, :] = f
        for i, value in enumerate((p, m, f)):
            put_rows(send1, i, value, x)
        return total + m, z_pack(pack_p, p, x), z_pack(pack_m, m, x), z_pack(pack_f, f, x)

    total, *packed = sweep(stage_a, (zero, zero, zero, zero))
    mean = jnp.sum(jnp.sum(total, axis=0, keepdims=True), axis=1, keepdims=True) * (
        1.0 / (CX * CY * CZ)
    )
    inv_mean = 1.0 / mean

    pl.semaphore_wait(barrier, len(everyone))
    round1 = exchange(send1, recv1, (press, mob, frac0), packed)
    for copy in loads[4:]:
        copy.wait()

    def harmonic(a, b):
        return 2.0 * a * b / (a + b)

    def x_face(x):
        tx = harmonic(mid(mob, x), mid(mob, x + 1))
        fx = tx * (mid(press, x) - mid(press, x + 1))
        trans_x[x] = tx
        flux_x[x] = fx
        return fx

    def stage_b(x, before):
        fx = x_face(x + 1)
        ty = harmonic(mob[x + 1, 0:40, :], mob[x + 1, 1:41, :])
        fy = ty * (press[x + 1, 0:40, :] - press[x + 1, 1:41, :])
        trans_y[x] = ty
        flux_y[x] = fy
        m = mid(mob, x + 1)
        p = mid(press, x + 1)
        tz = jnp.where(lane == CZ - 1, 0.0, harmonic(m, pltpu.roll(m, CZ - 1, 1)))
        fz = tz * (p - pltpu.roll(p, CZ - 1, 1))
        trans_z[x] = tz
        flux_z[x] = fz
        diag = comp[x] + WELL_INDEX * wells[x].astype(F32) * m
        comp[x] = diag
        result = diag * p + (fx - before)
        result = result + (fy[8:40] - flux_y[x, 7:39, :])
        result = result + (fz - pltpu.roll(fz, 1, 1))
        box[x + W, W : W + CY, :] = src[x] - result
        return fx

    sweep(stage_b, x_face(0))
    for copy in round1:
        copy.wait()
    for k in range(5):
        own_p, own_m = (send1[k, i * CX : (i + 1) * CX, :] for i in range(2))
        far_p, far_m = (recv1[k, i * CX : (i + 1) * CX, :] for i in range(2))
        tk = harmonic(own_m, far_m)
        if k == 4:
            tk = jnp.where(lane < CX, tk, 0.0)
        face_t[k] = tk
        face_p[k] = tk * (own_p - far_p)

    def stage_r(x, carry):
        big = x + W
        r = box[big, W : W + CY, :] - at_faces(face_p, x)
        box[big, W : W + CY, :] = r
        group = big // 16
        place = (big % 16) * 8
        moved = pltpu.roll(r, lax.rem(place + 8 * (1 - layer), CZ), 1)
        kept = rz_send[group, W : W + CY, :]
        rz_send[group, W : W + CY, :] = jnp.where(
            (lane >= place) & (lane < place + 8), moved, kept
        )
        return carry

    inside = pl.ds(W, CX)
    cut = {-1: (pl.ds(W, W), pl.ds(W + CX, W)), 0: (inside, inside), 1: (pl.ds(CX, W), pl.ds(0, W))}
    wide_copies, far_copies = [], []
    for dx in (-1, 1, 0):
        for dy in (0, -1, 1):
            (sx, tx), (sy, ty) = cut[dx], cut[dy]
            if dx or dy:
                wide_copies.append(remote(box.at[sx, sy], box.at[tx, ty], device(dx, dy, 0)))
            if dx:
                mine, theirs = (0, 1) if dx < 0 else (2, 0)
                source_ref, target_ref = rz_send.at[mine, sy], rxz.at[theirs, ty]
            else:
                source_ref, target_ref = rz_send.at[:, sy], rz.at[:, ty]
            far_copies.append(remote(source_ref, target_ref, device(dx, dy, 1)))
    for k in range(2):
        lax.fori_loop(24 * k, 24 * k + 8, stage_r, 0, unroll=8)
        wide_copies[3 * k].start()
    lax.fori_loop(8, 24, stage_r, 0, unroll=16)
    for copy in far_copies[6:7] + wide_copies[6:] + far_copies[:6] + far_copies[7:] + wide_copies[1:3] + wide_copies[4:6]:
        copy.start()
    for copy in wide_copies:
        copy.wait()

    wide_lane = lax.broadcasted_iota(jnp.int32, (BY, CZ), 1)

    def fold(i, carry):
        j = BX - 1 - i
        v, w = box[i], box[j]
        for parity, main in enumerate((v + w, v - w)):
            rows = pl.ds(pl.multiple_of((parity * HALF + i) * BY, 16), BY)
            high, low = split(main)
            a_hi[rows, :] = high
            a_lo[rows, :] = low
        return carry

    sweep(fold, 0, HALF, 8)
    for copy in const_loads:
        copy.wait()
    weights2 = wz2[layer]
    for chunk in range(6):
        rows = slice(chunk * 384, (chunk + 1) * 384)
        high = a_hi[rows]
        out = mm(jnp.concatenate([high, a_lo[rows]], axis=1), wz1[...]) + mm(high, weights2[:CZ])
        z1[chunk // 3, (chunk % 3) * 8 : (chunk % 3) * 8 + 8] = out.reshape(8, BY, CPAD)
    for copy in far_copies:
        copy.wait()
    own_left = wide_lane < CZ // 2
    rz_all[0] = jnp.where(own_left, rxz[0], rz[0])
    rz_all[1] = rz[1]
    rz_all[2] = jnp.where(own_left, rz[2], rxz[1])

    def fold_far(i, carry):
        j = BX - 1 - i
        hv = pltpu.roll(rz_all[i // 16], lax.rem(CZ - (i % 16) * 8, CZ), 1)
        hw = pltpu.roll(rz_all[j // 16], lax.rem(CZ - (j % 16) * 8, CZ), 1)
        for parity, halo in enumerate((hv + hw, hv - hw)):
            rows = pl.ds(pl.multiple_of((parity * HALF + i) * BY, 16), BY)
            halo_high = halo.astype(BF16).astype(F32)
            halo_low = halo - halo_high
            tile = jnp.where(
                wide_lane < 8,
                halo_high,
                jnp.where(
                    wide_lane < 16, pltpu.roll(halo_low, 8, 1), pltpu.roll(halo_high, 16, 1)
                ),
            )
            a_halo[rows, :] = tile.astype(BF16)
        return carry

    sweep(fold_far, 0, HALF, 24)
    for chunk in range(6):
        rows = slice(chunk * 384, (chunk + 1) * 384)
        planes = slice((chunk % 3) * 8, (chunk % 3) * 8 + 8)
        out = mm(a_halo[rows], weights2[CZ:]).reshape(8, BY, CPAD)
        z1[chunk // 3, planes] = z1[chunk // 3, planes] + out
    for parity in range(2):
        for block in range(BY // 8):
            rows = slice(block * 8, block * 8 + 8)
            value = z1[parity, :, rows, :].reshape(HALF * 8, CPAD)
            out = mm_const(cx[parity], HALF * 8, value)
            x1[parity, :, rows, :] = out.reshape(HALF, 8, CPAD)
    for parity in range(2):
        for block in range(HALF // 4):
            span = slice(block * 4, block * 4 + 4)
            value = x1[parity, span].reshape(4 * BY, CPAD)
            out = mm_const(cy[...], 4 * BY, value) * inv[parity, span].reshape(4 * BY, CPAD)
            z1[parity, span] = out.reshape(4, BY, CPAD)
    for parity in range(2):
        for block in range(HALF // 4):
            span = slice(block * 4, block * 4 + 4)
            out = mm_const(cyb[...], 4 * CY, z1[parity, span].reshape(4 * BY, CPAD))
            y1[parity, span] = out.reshape(4, CY, CPAD)
    for parity in range(2):
        for block in range(CY // 8):
            rows = slice(block * 8, block * 8 + 8)
            value = y1[parity, :, rows, :].reshape(HALF * 8, CPAD)
            out = mm_const(cxb[parity], KEPT * 8, value)
            w1[parity, :, rows, :] = out.reshape(KEPT, 8, CPAD)
    for block in range(4):
        span = slice(block * 4, block * 4 + 4)
        sides = []
        for parity in range(2):
            high, low = split(w1[parity, span].reshape(4 * CY, CPAD))
            sides.append(mm(high, wzb[0]) + mm(low, wzb[0]) + mm(high, wzb[1]))
        plus = (sides[0] + sides[1]) * inv_mean
        minus = (sides[0] - sides[1]) * inv_mean
        for k in range(4):
            i = block * 4 + k
            direc[1 + i, 8 : 8 + CY, :] = plus[k * CY : (k + 1) * CY]
            direc[CX - i, 8 : 8 + CY, :] = minus[k * CY : (k + 1) * CY]

    def stage_c(x, carry):
        along, pack_d = carry
        d = mid(direc, x + 1)
        put_rows(send3, 0, d, x)
        return along + d * box[x + W, W : W + CY, :], z_pack(pack_d, d, x)

    along, pack_d = sweep(stage_c, (zero, zero), CX, 32)
    round3 = exchange(send3, recv3, (direc,), (pack_d,))

    def d_face(x):
        fx = trans_x[x] * (mid(direc, x) - mid(direc, x + 1))
        dflux_x[x] = fx
        return fx

    def stage_d(x, carry):
        before, curve = carry
        fx = d_face(x + 1)
        fy = trans_y[x] * (direc[x + 1, 0:40, :] - direc[x + 1, 1:41, :])
        dflux_y[x] = fy
        d = mid(direc, x + 1)
        fz = trans_z[x] * (d - pltpu.roll(d, CZ - 1, 1))
        dflux_z[x] = fz
        result = comp[x] * d + (fx - before)
        result = result + (fy[8:40] - dflux_y[x, 7:39, :])
        result = result + (fz - pltpu.roll(fz, 1, 1))
        image[x] = result
        return fx, curve + d * result

    _, curve = sweep(stage_d, (d_face(0), zero))
    for copy in round3:
        copy.wait()
    for k in range(5):
        fd = face_t[k] * (send3[k] - recv3[k])
        face_d[k] = fd
        curve = curve + send3[k] * fd

    ar_send1[...] = jnp.concatenate(
        [
            jnp.broadcast_to(jnp.sum(value, axis=0, keepdims=True), (4, CZ))
            for value in (along, curve)
        ],
        axis=0,
    )

    def finish_image(x, carry):
        image[x] = image[x] + at_faces(face_d, x)
        return carry

    def prepare(x, carry):
        poro[x] = poro[x] / TIME_STEP
        perm[x] = INJECT_RATE * wells[x].astype(F32)
        outflow[x] = jnp.abs(fraction(sat[x], oil[x])[1])
        return carry

    for send, recv, peers in ((ar_send1, ar_recv2, peers2), (ar_send2, ar_recv1, peers1)):
        copies = [remote(send, recv.at[i], peer) for i, peer in enumerate(peers)]
        for copy in copies:
            copy.start()
        sweep(finish_image if send is ar_send1 else prepare, 0)
        for copy in copies:
            copy.wait()
        result = send[...]
        for i in range(len(peers)):
            result = result + recv[i]
        if send is ar_send1:
            ar_send2[...] = result
    sums = jnp.sum(result, axis=1, keepdims=True)
    step = sums[0:1] / sums[4:5]

    own_f, far_f = part(send1, 2), part(recv1, 2)
    for k in range(5):
        flux = face_p[k] + step * face_d[k]
        face_p[k] = flux
        face_o[k] = jnp.maximum(flux, 0.0)
        face_f[k] = upwind(flux, own_f[k], far_f[k])

    def total_x(x):
        fx = flux_x[x] + step * dflux_x[x]
        flux_x[x] = fx
        return fx, upwind(fx, mid(frac0, x), mid(frac0, x + 1))

    def balance_of(frac, fx_flow, flow_before, x):
        f = mid(frac, x + 1)
        flow_low = upwind(flux_y[x, 7:39, :], frac[x + 1, 7:39, :], f)
        flow_high = upwind(flux_y[x, 8:40, :], f, frac[x + 1, 9:41, :])
        flow_z = upwind(flux_z[x], f, pltpu.roll(f, CZ - 1, 1))
        balance = (fx_flow - flow_before) + (flow_high - flow_low)
        balance = balance + (flow_z - pltpu.roll(flow_z, 1, 1))
        return balance - perm[x]

    def inverse_of(storage, out_vals, sat_vals, oil_vals):
        _, slope = fraction(sat_vals, oil_vals)
        return 1.0 / (storage + out_vals * jnp.abs(slope))

    def stage_e(x, carry):
        fx_before, flow_before, pack_f = carry
        d = mid(direc, x + 1)
        press[x + 1, 8 : 8 + CY, :] = mid(press, x + 1) + step * d
        src[x] = box[x + W, W : W + CY, :] - step * image[x]
        fx, flow = total_x(x + 1)
        flux_y[x] = flux_y[x] + step * dflux_y[x]
        fz = flux_z[x] + step * dflux_z[x]
        flux_z[x] = fz
        out_vals = jnp.maximum(fx, 0.0) + jnp.maximum(-fx_before, 0.0)
        out_vals = out_vals + jnp.maximum(flux_y[x, 8:40, :], 0.0)
        out_vals = out_vals + jnp.maximum(-flux_y[x, 7:39, :], 0.0)
        out_vals = out_vals + jnp.maximum(fz, 0.0) + jnp.maximum(-pltpu.roll(fz, 1, 1), 0.0)
        out_vals = out_vals + at_faces(face_o, x)
        slope = outflow[x]
        outflow[x] = out_vals
        s = sat[x]
        balance = balance_of(frac0, flow, flow_before, x) + at_faces(face_f, x)
        s_new = s - balance * (1.0 / (poro[x] + out_vals * slope))
        sat_b[x] = s_new
        f_new, _ = fraction(s_new, oil[x])
        frac1[x + 1, 8 : 8 + CY, :] = f_new
        put_rows(send4, 0, f_new, x)
        return fx, flow, z_pack(pack_f, f_new, x)

    fx, flow = total_x(0)
    _, _, pack_f = sweep(stage_e, (fx, flow, zero))
    round4 = exchange(send4, recv4, (frac1,), (pack_f,))
    stores = [
        pltpu.make_async_copy(press.at[inner], pressure_out, out_sems.at[0]),
        pltpu.make_async_copy(src, residual_out, out_sems.at[1]),
    ]
    for copy in stores:
        copy.start()

    def within(frac, x, flow_before):
        flow = upwind(flux_x[x + 1], mid(frac, x + 1), mid(frac, x + 2))
        storage = poro[x]
        s = sat_b[x]
        balance = balance_of(frac, flow, flow_before, x) + storage * (s - sat[x])
        inverse = inverse_of(storage, outflow[x], s, oil[x])
        image[x] = inverse
        sat_b[x] = s - balance * inverse
        return flow

    def across(last, x, pack_f):
        s_new = sat_b[x] - at_faces(face_f, x) * image[x]
        sat_b[x] = s_new
        if last:
            return pack_f
        f_new, _ = fraction(s_new, oil[x])
        frac2[x + 1, 8 : 8 + CY, :] = f_new
        put_rows(send5, 0, f_new, x)
        return z_pack(pack_f, f_new, x)

    def later(frac, send, recv, copies, last):
        sweep(functools.partial(within, frac), zero)
        for copy in copies:
            copy.wait()
        for k in range(5):
            face_f[k] = upwind(face_p[k], send[k], recv[k])
        return sweep(functools.partial(across, last), zero, CX, 32)

    pack_f = later(frac1, send4, recv4, round4, False)
    round5 = exchange(send5, recv5, (frac2,), (pack_f,))
    later(frac2, send5, recv5, round5, True)
    last_store = pltpu.make_async_copy(sat_b, saturation_out, out_sems.at[2])
    last_store.start()
    for copy in (*stores, last_store):
        copy.wait()


def per_device(sizes, *args):
    consts = tables()
    brick = pltpu.VMEM((CX, CY, CZ), F32)
    bricki = pltpu.VMEM((CX, CY, CZ), jnp.int32)
    padded = pltpu.VMEM((CX + 2, BY, CZ), F32)
    faces_x = pltpu.VMEM((CX + 1, CY, CZ), F32)
    faces_y = pltpu.VMEM((CX, 40, CZ), F32)

    def buffers(fields):
        return [pltpu.VMEM((5, fields * CX, CZ), F32)] * 2

    rows = 2 * HALF * BY
    n1 = sizes[0] * sizes[2] - 1
    n2 = sizes[1] - 1
    tile = pltpu.VMEM((8, CZ), F32)
    n_remote = 5 * 4 + 17 + n1 + n2
    scratch = (
        [padded, brick, brick, brick, brick, brick, bricki, bricki]
        + [pltpu.VMEM(c.shape, c.dtype) for c in consts]
        + [padded] * 4
        + [brick, padded, brick]
        + [faces_x, faces_y, brick] * 3
        + [brick] * 2
        + buffers(3)
        + buffers(1) * 3
        + [pltpu.VMEM((BX, BY, CZ), F32)]
        + [pltpu.VMEM((3, BY, CZ), F32)] * 3
        + [pltpu.VMEM((2, BY, CZ), F32)]
        + [pltpu.VMEM((rows, CZ), BF16)] * 3
        + [pltpu.VMEM((2, HALF, BY, CPAD), F32)] * 2
        + [pltpu.VMEM((2, HALF, CY, CPAD), F32), pltpu.VMEM((2, KEPT, CY, CPAD), F32)]
        + [pltpu.VMEM((5, CY, CZ), F32)] * 5
        + [tile, pltpu.VMEM((n1, 8, CZ), F32), tile, pltpu.VMEM((n2, 8, CZ), F32)]
        + [pltpu.SemaphoreType.DMA((8,)), pltpu.SemaphoreType.DMA((8,))]
        + [pltpu.SemaphoreType.DMA((3,))]
        + [pltpu.SemaphoreType.DMA((n_remote,))] * 2
    )
    anywhere = pl.BlockSpec(memory_space=pl.ANY)
    in_specs = [anywhere] * 8 + [pl.BlockSpec(memory_space=pltpu.SMEM)] + [anywhere] * len(consts)
    results = pl.pallas_call(
        functools.partial(kernel, sizes),
        out_shape=[jax.ShapeDtypeStruct((CX, CY, CZ), F32)] * 3,
        in_specs=in_specs,
        out_specs=[anywhere] * 3,
        scratch_shapes=scratch,
        compiler_params=pltpu.CompilerParams(
            collective_id=0, has_side_effects=True, vmem_limit_bytes=60 * 1024 * 1024
        ),
    )(*args, *(jnp.asarray(c) for c in consts))

    whole = pl.BlockSpec((CX, CY, CZ), lambda: (0, 0, 0))
    return pl.pallas_call(
        handed_on,
        out_shape=[jax.ShapeDtypeStruct((CX, CY, CZ), F32)] * 3,
        in_specs=[whole] * 3,
        out_specs=[whole] * 3,
    )(*results)


def handed_on(*refs):
    for i in range(3):
        refs[3 + i][...] = refs[i][...]


def solution(mesh):
    sizes = tuple(mesh.shape[axis] for axis in ("gx", "gy", "gz"))
    spec = P("gx", "gy", "gz")
    return jax.shard_map(
        functools.partial(per_device, sizes),
        mesh=mesh,
        in_specs=(spec,) * 8 + (P(),),
        out_specs=(spec,) * 3,
        check_vma=False,
    )
```
